512 devices in a mesh: dp: 32 (over y_lo, z, core), pipe: 16 (over x, y_hi).
Axes of the slice: x: 4, y: 8 (y_hi: 4, y_lo: 2; y = y_hi * 2 + y_lo), z: 8, core: 2. Of those that a mesh axis runs over, the one named last changes fastest.
Arguments:
- encoder_out: bfloat16 [2048, 8192], P('pipe', 'dp'), may hold values from -6 to 6
- key_value_weight: bfloat16 [16, 2048, 2048], P('pipe', 'dp'), may hold values from -0.125 to 0.125
- queries: bfloat16 [16, 8192, 1024], P('pipe', 'dp'), may hold values from -1.1953125 to 1.1953125
- context_gradient: bfloat16 [16, 8192, 1024], P('pipe', 'dp'), may hold values from -6 to 6
Outputs:
- context: bfloat16 [16, 8192, 1024], P('pipe', 'dp')
- grad_encoder: bfloat16 [2048, 8192], P('pipe', 'dp')
The draws below stay inside these ranges and needn't reach their ends.
All inputs are finite; a program needn't handle non-finite values.
Results may differ from the reference program's by a relative error of at most 0.02.
Values may be sent and summed in bfloat16 or wider, within the bound.
A program may use at most 64 MiB of HBM per device.

```python
import jax
import jax.numpy as jnp
from jax import lax

MODEL_WIDTH = 2048
LOCAL_HEADS = 8
HEAD_WIDTH = 128
ENCODER_LENGTH = 128
DECODER_LENGTH = 128
KEY_WIDTH = 1024
TOKENS = 8192
DECODER_TOKENS = 8192
DECODER_SECTIONS = 16


def levels(rng, shape, split, smallest, top_value):
    factor_of = 1.0
    for dim, parts in split:
        heights = jax.random.uniform(jax.random.fold_in(jax.random.fold_in(rng, 6), dim), (parts,), jnp.float32, smallest / len(split), top_value / len(split))
        factor_of = factor_of * jnp.repeat(jnp.exp(heights), shape[dim] // parts).reshape((-1,) + (1,) * (len(shape) - 1 - dim))
    return factor_of


def bell_draw(rng, shape, width, bound, split=(), kind=jnp.bfloat16):
    entries = jax.random.normal(rng, shape, jnp.float32) * width
    if len(split) > 0:
        entries = levels(rng, shape, split, -0.22, 0.18) * entries
    return jnp.clip(entries, min=-bound, max=bound).astype(kind)


def setup_inputs(seed: int = 0) -> dict:
    streams_of = jax.random.split(jax.random.key(seed), 5)
    encoder_out = bell_draw(streams_of[0], (MODEL_WIDTH, TOKENS), 1.0, 6.0, ((0, 16), (1, 32)))
    key_value_weight = bell_draw(streams_of[1], (DECODER_SECTIONS, MODEL_WIDTH, 2 * KEY_WIDTH), MODEL_WIDTH ** -0.5, 0.125, ((0, 16), (1, 32)))
    queries = bell_draw(streams_of[2], (DECODER_SECTIONS, DECODER_TOKENS, KEY_WIDTH), 0.2, 1.1953125, ((0, 16), (1, 32)))
    context_gradient = bell_draw(streams_of[3], (DECODER_SECTIONS, DECODER_TOKENS, KEY_WIDTH), 1.0, 6.0, ((0, 16), (1, 32)))
    return dict(encoder_out=encoder_out, key_value_weight=key_value_weight, queries=queries, context_gradient=context_gradient)


def attend(query_rows, grad_rows, key_value_rows, row_count):
    key_rows = key_value_rows[:, :KEY_WIDTH].astype(jnp.float32).reshape(row_count, ENCODER_LENGTH, LOCAL_HEADS, HEAD_WIDTH)
    value_rows = key_value_rows[:, KEY_WIDTH:].astype(jnp.float32).reshape(row_count, ENCODER_LENGTH, LOCAL_HEADS, HEAD_WIDTH)
    query = query_rows.astype(jnp.float32).reshape(row_count, DECODER_LENGTH, LOCAL_HEADS, HEAD_WIDTH)
    upstream = grad_rows.astype(jnp.float32).reshape(row_count, DECODER_LENGTH, LOCAL_HEADS, HEAD_WIDTH)
    scores = jnp.einsum("bqhd,bkhd->bhqk", query, key_rows)
    probs = jax.nn.softmax(scores, axis=-1)
    probs_bf = probs.astype(jnp.bfloat16).astype(jnp.float32)
    context = jnp.einsum("bhqk,bkhd->bqhd", probs_bf, value_rows).astype(jnp.bfloat16)
    grad_probs = jnp.einsum("bqhd,bkhd->bhqk", upstream, value_rows)
    inner = jnp.sum(grad_probs * probs, axis=-1, keepdims=True)
    grad_scores = (probs * (grad_probs - inner)).astype(jnp.bfloat16).astype(jnp.float32)
    key_gradient = jnp.einsum("bhqk,bqhd->bkhd", grad_scores, query).astype(jnp.bfloat16)
    value_gradient = jnp.einsum("bhqk,bqhd->bkhd", probs_bf, upstream).astype(jnp.bfloat16)
    key_value_gradient = jnp.concatenate([key_gradient.reshape(row_count * ENCODER_LENGTH, KEY_WIDTH), value_gradient.reshape(row_count * ENCODER_LENGTH, KEY_WIDTH)], axis=1)
    return context.reshape(row_count * DECODER_LENGTH, KEY_WIDTH), key_value_gradient


def reference(encoder_out, key_value_weight, queries, context_gradient):
    row_count = TOKENS // ENCODER_LENGTH

    def section_step(total, inputs):
        weight, query_rows, grad_rows = inputs
        key_value_rows = jnp.dot(encoder_out.T, weight, preferred_element_type=jnp.float32).astype(jnp.bfloat16)
        context, key_value_gradient = attend(query_rows, grad_rows, key_value_rows, row_count)
        total = total + jnp.dot(weight, key_value_gradient.T, preferred_element_type=jnp.float32)
        return total, context

    start = jnp.zeros((MODEL_WIDTH, TOKENS), jnp.float32)
    total, context = lax.scan(section_step, start, (key_value_weight, queries, context_gradient))
    return context, total.astype(jnp.bfloat16)
```

```python
import jax
import jax.numpy as jnp
from jax import lax
from jax.experimental import pallas as pl
from jax.experimental.pallas import tpu as pltpu
from jax.sharding import PartitionSpec as P

MESH = pl.DeviceIdType.MESH
HEADS = 8
HD = 128
SEQ = 128
TOK = 256
WIDTH = 2048
NZ = 8
F32 = jnp.float32
BF16 = jnp.bfloat16


def nt(a, b):
    return lax.dot_general(a, b, (((1,), (1,)), ((), ())), preferred_element_type=F32)


def nn(a, b):
    return lax.dot_general(a, b, (((1,), (0,)), ((), ())), preferred_element_type=F32)


def kernel(
    enc_ref, w_ref, q_ref, cg_ref, ctx_ref, ge_ref,
    wb, w_st, enc_buf, enc_t, acc, q_v, cg_v, ctx_v, kv_v, gkv_v, xs, xr, ys, yr,
    loc, ring_s, ring_r, wy_s, wy_r, sib_s, sib_r, enc_s, enc_r, gx_s, gx_r, gy_s, gy_r,
):
    dp, pipe = lax.axis_index("dp"), lax.axis_index("pipe")
    core, z, row = dp % 2, (dp // 2) % NZ, dp // (2 * NZ)
    x, y = pipe // 4, pipe % 4
    dz = 1 - 2 * core
    orow = 1 - row

    def at_z(k):
        return (z + k * dz + 2 * NZ) % NZ

    def dp_of(r, zz, c):
        return {"dp": (r * NZ + zz) * 2 + c}

    def pipe_of(xx, yy):
        return {"pipe": xx * 4 + yy}

    far, near = dp_of(row, at_z(1), core), dp_of(row, at_z(-1), core)
    mate = dp_of(orow, z, core)
    twin = dp_of(row, z, 1 - core)
    xp, xm, xo = (x + 1) % 4, (x + 3) % 4, (x + 2) % 4
    yp, ym, yo = (y + 1) % 4, (y + 3) % 4, (y + 2) % 4
    x_up, x_dn = pipe_of(xp, y), pipe_of(xm, y)
    y_up, y_dn = pipe_of(x, yp), pipe_of(x, ym)

    started = []

    def send(src, dst, ss, rs, dev):
        c = pltpu.make_async_remote_copy(
            src_ref=src, dst_ref=dst, send_sem=ss, recv_sem=rs, device_id=dev, device_id_type=MESH
        )
        c.start()
        started.append(c)

    def arrived(dst, ss, rs, dev):
        pltpu.make_async_remote_copy(
            src_ref=dst, dst_ref=dst, send_sem=ss, recv_sem=rs, device_id=dev, device_id_type=MESH
        ).wait_recv()

    in_enc = pltpu.make_async_copy(enc_ref, enc_buf.at[:, pipe], loc.at[0])
    in_w = pltpu.make_async_copy(w_ref, w_st, loc.at[1])
    in_q = pltpu.make_async_copy(q_ref, q_v, loc.at[2])
    in_cg = pltpu.make_async_copy(cg_ref, cg_v, loc.at[3])
    in_enc.start()
    in_w.start()
    in_q.start()
    in_cg.start()

    barrier = pltpu.get_barrier_semaphore()
    for dev in (far, near, mate, twin, x_up, x_dn, y_up, y_dn):
        pl.semaphore_signal(barrier, inc=1, device_id=dev, device_id_type=MESH)
    pl.semaphore_wait(barrier, 8)

    groups = [("a", 0, 2), ("a", 2, 2), ("b", 4, 1), ("b", 5, 1), ("b", 6, 1), ("b", 7, 1)]

    def piece(g, zz):
        kind, h0, n = groups[g]
        if kind == "a":
            return wb.at[pl.ds(h0, n), core, row, zz]
        return wb.at[h0, core, :, zz]

    def rearrange(h):
        wb[h, core, row, z, :, :HD] = w_st[:, h * HD : (h + 1) * HD]
        wb[h, core, row, z, :, HD:] = w_st[:, (HEADS + h) * HD : (HEADS + h + 1) * HD]

    def mate_send(k, src):
        send(src, src, wy_s.at[k], wy_r.at[k], mate)

    def a_first(i, zz):
        s = wb.at[0, core, row, zz]
        mate_send(i, s)

    def ring(g, k):
        kind, h0, n = groups[g]
        if k >= 1:
            p = piece(g, at_z(-k))
            arrived(p, ring_s.at[g, k - 1], ring_r.at[g, k - 1], near)
            if k <= 3:
                p = piece(g, at_z(k))
                arrived(p, ring_s.at[g, 3 + k], ring_r.at[g, 3 + k], far)
        if k <= 3:
            p = piece(g, at_z(-k))
            send(p, p, ring_s.at[g, k], ring_r.at[g, k], far)
        if k <= 2:
            p = piece(g, at_z(k))
            send(p, p, ring_s.at[g, 4 + k], ring_r.at[g, 4 + k], near)
        if g == 0:
            a_first(k, at_z(-k))
            if 1 <= k <= 3:
                a_first(4 + k, at_z(k))
        if g == 5:
            p = piece(g, at_z(-k))
            send(p, p, sib_s.at[10 + k], sib_r.at[10 + k], twin)
            if 1 <= k <= 3:
                p = piece(g, at_z(k))
                send(p, p, sib_s.at[14 + k], sib_r.at[14 + k], twin)
        elif k == 4:
            if kind == "a":
                for h in range(max(h0, 1), h0 + n):
                    mate_send(7 + h, wb.at[h, core, row])
                p = wb.at[pl.ds(h0, n), core, row]
            else:
                p = wb.at[h0, core]
            send(p, p, sib_s.at[g], sib_r.at[g], twin)

    def mate_done(h):
        if h == 0:
            for i in range(8):
                zz = at_z(-i) if i <= 4 else at_z(i - 4)
                arrived(wb.at[0, core, orow, zz], wy_s.at[i], wy_r.at[i], mate)
        else:
            arrived(wb.at[h, core, orow], wy_s.at[7 + h], wy_r.at[7 + h], mate)
        p = wb.at[h, core, orow]
        send(p, p, sib_s.at[6 + h], sib_r.at[6 + h], twin)

    oc = 1 - core

    def twin_own(g):
        kind, h0, n = groups[g]
        if kind == "a":
            p = wb.at[pl.ds(h0, n), oc, row]
        else:
            p = wb.at[h0, oc]
        arrived(p, sib_s.at[g], sib_r.at[g], twin)

    def twin_done(h):
        if h < 4:
            arrived(wb.at[h, oc, orow], sib_s.at[6 + h], sib_r.at[6 + h], twin)
        elif h < 7:
            twin_own(h - 2)
        else:
            for k in range(5):
                arrived(wb.at[7, oc, :, (z + k * dz + 2 * NZ) % NZ], sib_s.at[10 + k], sib_r.at[10 + k], twin)
            for k in range(1, 4):
                arrived(wb.at[7, oc, :, at_z(-k)], sib_s.at[14 + k], sib_r.at[14 + k], twin)

    def enc_x(yy, i):
        b = enc_buf.at[:, x * 4 + yy]
        send(b, b, enc_s.at[4 + i], enc_r.at[4 + i], x_up)
        send(b, b, enc_s.at[8 + i], enc_r.at[8 + i], x_dn)

    def enc_x2(yy, i):
        b = enc_buf.at[:, xm * 4 + yy]
        arrived(b, enc_s.at[4 + i], enc_r.at[4 + i], x_dn)
        b = b.at[0]
        send(b, b, enc_s.at[12 + i], enc_r.at[12 + i], x_up)
        b = enc_buf.at[:, xp * 4 + yy]
        arrived(b, enc_s.at[8 + i], enc_r.at[8 + i], x_up)
        b = b.at[1]
        send(b, b, enc_s.at[16 + i], enc_r.at[16 + i], x_dn)

    def enc_0():
        b = enc_buf.at[:, pipe]
        send(b, b, enc_s.at[0], enc_r.at[0], y_up)
        send(b, b, enc_s.at[1], enc_r.at[1], y_dn)
        enc_x(y, 0)

    def enc_1():
        b = enc_buf.at[:, x * 4 + ym]
        arrived(b, enc_s.at[0], enc_r.at[0], y_dn)
        b = b.at[0]
        send(b, b, enc_s.at[2], enc_r.at[2], y_up)
        b = enc_buf.at[:, x * 4 + yp]
        arrived(b, enc_s.at[1], enc_r.at[1], y_up)
        b = b.at[1]
        send(b, b, enc_s.at[3], enc_r.at[3], y_dn)
        enc_x(ym, 1)
        enc_x(yp, 2)

    def enc_2():
        arrived(enc_buf.at[0, x * 4 + yo], enc_s.at[2], enc_r.at[2], y_dn)
        arrived(enc_buf.at[1, x * 4 + yo], enc_s.at[3], enc_r.at[3], y_up)
        enc_x(yo, 3)

    def enc_end():
        for i, yy in enumerate((y, ym, yp, yo)):
            arrived(enc_buf.at[0, xo * 4 + yy], enc_s.at[12 + i], enc_r.at[12 + i], x_dn)
            arrived(enc_buf.at[1, xo * 4 + yy], enc_s.at[16 + i], enc_r.at[16 + i], x_up)

    def transpose(c):
        b = enc_buf[c // 2, (c % 2) * 8 : (c % 2) * 8 + 8]
        enc_t[:, c * 512 : (c + 1) * 512] = b.reshape(512, TOK).T

    def project(h):
        w = wb[h].reshape(WIDTH, 2 * HD)
        kv_v[...] = nn(enc_t[...], w).astype(BF16)

    def attend(h, i):
        rows = slice(i * SEQ, (i + 1) * SEQ)
        cols = slice(h * HD, (h + 1) * HD)
        k, v = kv_v[rows, :HD], kv_v[rows, HD:]
        q, cg = q_v[rows, cols], cg_v[rows, cols]
        s = nt(k, q)
        e = jnp.exp(s - jnp.max(s, axis=0, keepdims=True))
        p = e / jnp.sum(e, axis=0, keepdims=True)
        pb = p.astype(BF16)
        ctx_v[rows, cols] = nn(pb.T, v).astype(BF16)
        gp = nt(v, cg)
        inner = jnp.sum(gp * p, axis=0, keepdims=True)
        gs = (p * (gp - inner)).astype(BF16)
        gkv_v[rows, :HD] = nn(gs, q).astype(BF16)
        gkv_v[rows, HD:] = nn(pb, cg).astype(BF16)

    def grad(h):
        g = gkv_v[...]
        for c in range(4):
            j, r = c // 2, c % 2
            t = nt(wb[h, j, r].reshape(512, 2 * HD), g).reshape(NZ, 64, TOK)
            acc[j, r] = t if first[0] else acc[j, r] + t
        first[0] = False

    first = [True]

    def head(h, during=()):
        twin_done(h)
        project(h)
        for f in during[:1]:
            f()
        attend(h, 0)
        attend(h, 1)
        for f in during[1:2]:
            f()
        grad(h)
        for f in during[2:]:
            f()

    in_enc.wait()
    enc_0()
    in_w.wait()
    rearrange(0)
    rearrange(1)
    ring(0, 0)
    rearrange(2)
    rearrange(3)
    ring(1, 0)
    for h in range(4, 8):
        rearrange(h)
    p = wb.at[pl.ds(4, 4), core, row, z]
    mate_send(11, p)
    enc_1()
    ring(0, 1)
    enc_x2(y, 0)
    ring(1, 1)
    enc_2()
    ring(0, 2)
    enc_x2(ym, 1)
    enc_x2(yp, 2)
    ring(1, 2)
    arrived(wb.at[pl.ds(4, 4), core, orow, z], wy_s.at[11], wy_r.at[11], mate)
    ring(2, 0)
    ring(0, 3)
    enc_x2(yo, 3)
    ring(1, 3)
    ring(2, 1)
    ring(0, 4)
    ring(3, 0)
    ring(1, 4)
    enc_end()
    in_q.wait()
    in_cg.wait()
    transpose(0)
    transpose(1)
    ring(2, 2)
    transpose(2)
    transpose(3)
    ring(3, 1)
    mate_done(0)
    ring(2, 3)
    twin_own(0)
    head(0, (lambda: ring(3, 2), lambda: ring(4, 0), lambda: ring(2, 4)))
    ring(3, 3)
    ring(4, 1)
    mate_done(1)
    head(4, (lambda: ring(3, 4), lambda: ring(4, 2), lambda: ring(5, 0)))
    ring(4, 3)
    ring(5, 1)
    head(1, (lambda: ring(4, 4), lambda: mate_done(2), lambda: ring(5, 2)))
    head(5, (lambda: ring(5, 3),))
    twin_own(1)
    head(2)
    ring(5, 4)
    head(6)
    mate_done(3)
    head(3)

    twin_done(7)
    project(7)
    attend(7, 0)
    attend(7, 1)
    out_ctx = pltpu.make_async_copy(ctx_v, ctx_ref, loc.at[4])
    out_ctx.start()
    g7 = gkv_v[...]
    order = (yo, yp, ym, y)

    def blocks(ref, j, xx):
        return ref.at[j, xx // 2, pl.ds((xx % 2) * 4, 4)]

    def last(j, xx):
        w = blocks(wb.at[7], j, xx)[...].reshape(TOK, 2 * HD)
        return blocks(acc, j, xx)[...] + nt(w, g7).reshape(4, 64, TOK)

    def one(j, xx, yy):
        return acc.at[j, xx // 2, (xx % 2) * 4 + yy]

    def gx(m, r):
        send(xs.at[m, order[r]], xr.at[m, order[r]], gx_s.at[m, r], gx_r.at[m, r], x_up if m % 2 == 0 else x_dn)

    def gx_in(m, r):
        dev = x_dn if m % 2 == 0 else x_up
        arrived(xr.at[m, order[r]], gx_s.at[m, r], gx_r.at[m, r], dev)
        return xr[m, order[r]].astype(F32)

    for m, (j, xx) in enumerate(((0, xo), (1, xo), (1, xp), (0, xm))):
        xs[m] = last(j, xx).astype(BF16)
        if m in (1, 3):
            for r in range(4):
                gx(m - 1, r)
                gx(m, r)
    for j, xx in ((0, xp), (1, xm), (0, x), (1, x)):
        blocks(acc, j, xx)[...] = last(j, xx)
    for r in range(4):
        xs[4, order[r]] = (gx_in(0, r) + one(0, xp, order[r])[...]).astype(BF16)
        gx(4, r)
        xs[5, order[r]] = (gx_in(1, r) + one(1, xm, order[r])[...]).astype(BF16)
        gx(5, r)

    def total(r):
        t1 = one(1, x, order[r])[...] + gx_in(2, r)
        t0 = one(0, x, order[r])[...] + gx_in(3, r)
        return t0 + gx_in(4, r), t1 + gx_in(5, r)

    def gy(m, v):
        ys[m] = v.astype(BF16)
        send(ys.at[m], yr.at[m], gy_s.at[m], gy_r.at[m], y_up if m % 2 == 0 else y_dn)

    def gy_in(m):
        arrived(yr.at[m], gy_s.at[m], gy_r.at[m], y_dn if m % 2 == 0 else y_up)
        return yr[m].astype(F32)

    s0, s1 = total(0)
    gy(0, s0)
    gy(1, s1)
    u0, u1 = total(1)
    gy(2, u1)
    gy(4, u0 + gy_in(0))
    d0, d1 = total(2)
    gy(3, d0)
    gy(5, d1 + gy_in(1))
    o0, o1 = total(3)
    ge_ref[0] = (o0 + gy_in(3) + gy_in(4)).astype(BF16)
    ge_ref[1] = (o1 + gy_in(2) + gy_in(5)).astype(BF16)

    for c in started:
        c.wait_send()
    out_ctx.wait()


def local(encoder_out, key_value_weight, queries, context_gradient):
    any_space = pl.BlockSpec(memory_space=pl.ANY)
    vmem = pl.BlockSpec(memory_space=pltpu.VMEM)
    dma = pltpu.SemaphoreType.DMA
    ctx, ge = pl.pallas_call(
        kernel,
        out_shape=(
            jax.ShapeDtypeStruct((TOK, HEADS * HD), BF16),
            jax.ShapeDtypeStruct((2, 64, TOK), BF16),
        ),
        in_specs=[any_space] * 4,
        out_specs=(any_space, vmem),
        scratch_shapes=[
            pltpu.VMEM((HEADS, 2, 2, NZ, 64, 2 * HD), BF16),
            pltpu.VMEM((64, WIDTH), BF16),
            pltpu.VMEM((2, 16, 64, TOK), BF16),
            pltpu.VMEM((TOK, WIDTH), BF16),
            pltpu.VMEM((2, 2, NZ, 64, TOK), F32),
            pltpu.VMEM((TOK, HEADS * HD), BF16),
            pltpu.VMEM((TOK, HEADS * HD), BF16),
            pltpu.VMEM((TOK, HEADS * HD), BF16),
            pltpu.VMEM((TOK, 2 * HD), BF16),
            pltpu.VMEM((TOK, 2 * HD), BF16),
            pltpu.VMEM((6, 4, 64, TOK), BF16),
            pltpu.VMEM((6, 4, 64, TOK), BF16),
            pltpu.VMEM((6, 64, TOK), BF16),
            pltpu.VMEM((6, 64, TOK), BF16),
            dma((5,)),
            dma((6, 7)),
            dma((6, 7)),
            dma((12,)),
            dma((12,)),
            dma((18,)),
            dma((18,)),
            dma((20,)),
            dma((20,)),
            dma((6, 4)),
            dma((6, 4)),
            dma((6,)),
            dma((6,)),
        ],
        compiler_params=pltpu.CompilerParams(
            collective_id=0, has_side_effects=True, vmem_limit_bytes=48 * 1024 * 1024
        ),
    )(
        encoder_out.reshape(2, 64, TOK),
        key_value_weight[0],
        queries[0],
        context_gradient[0],
    )
    return ctx[None], ge.reshape(2 * 64, TOK)


def solution(mesh):
    return jax.shard_map(
        local,
        mesh=mesh,
        in_specs=(P("pipe", "dp"), P("pipe", "dp", None), P("pipe", "dp", None), P("pipe", "dp", None)),
        out_specs=(P("pipe", "dp", None), P("pipe", "dp")),
        check_vma=False,
    )
```

```python
import jax
import jax.numpy as jnp
from jax import lax
from jax.experimental import pallas as pl
from jax.experimental.pallas import tpu as pltpu
from jax.sharding import PartitionSpec as P

MESH = pl.DeviceIdType.MESH
HEADS = 8
HD = 128
SEQ = 128
TOK = 256
WIDTH = 2048
NZ = 8
LIMIT = 62
F32 = jnp.float32
BF16 = jnp.bfloat16

ORDER = [
    ("e0",), ("yb",), ("F", 0, 0), ("N", 0, 0), ("F", 1, 0), ("N", 1, 0), ("F", 0, 1), ("ex", 0), ("N", 0, 1),
    ("F", 1, 1), ("N", 1, 1), ("e1",), ("F", 0, 2), ("N", 0, 2), ("F", 1, 2), ("ybw",), ("F", 2, 0),
    ("N", 2, 0), ("N", 1, 2), ("ex", 1), ("F", 0, 3), ("N", 0, 3), ("F", 3, 0), ("N", 3, 0), ("ex", 2),
    ("F", 1, 3), ("F", 2, 1), ("N", 2, 1), ("e2",), ("N", 1, 3), ("F", 0, 4), ("F", 4, 0), ("N", 4, 0),
    ("end", 0), ("ys", 1), ("F", 3, 1), ("N", 3, 1), ("ex", 3), ("F", 1, 4), ("end", 1), ("ys", 2), ("yd", 0),
    ("ys", 3), ("F", 2, 2), ("N", 2, 2), ("F", 4, 1), ("ee",), ("t", 0), ("N", 4, 1), ("t", 1), ("t", 2),
    ("t", 3), ("F", 3, 2), ("P", 0), ("A", 0), ("N", 3, 2), ("G", 0), ("F", 2, 3), ("N", 2, 3), ("F", 5, 0),
    ("N", 5, 0), ("yd", 1), ("F", 4, 2), ("N", 4, 2), ("F", 3, 3), ("P", 1), ("A", 1), ("N", 3, 3), ("G", 1),
    ("F", 2, 4), ("end", 2), ("F", 5, 1), ("N", 5, 1), ("F", 4, 3), ("P", 4), ("yd", 2), ("N", 4, 3),
    ("A", 4), ("F", 3, 4), ("end", 3), ("G", 4), ("F", 5, 2), ("P", 2), ("A", 2), ("N", 5, 2), ("G", 2),
    ("F", 4, 4), ("end", 4), ("P", 5), ("A", 5), ("F", 5, 3), ("G", 5), ("N", 5, 3), ("P", 6), ("yd", 3),
    ("A", 6), ("G", 6), ("F", 5, 4), ("end", 5), ("P", 3), ("A", 3), ("G", 3), ("P", 7), ("A", 7),
]


def nt(a, b):
    return lax.dot_general(a, b, (((1,), (1,)), ((), ())), preferred_element_type=F32)


def nn(a, b):
    return lax.dot_general(a, b, (((1,), (0,)), ((), ())), preferred_element_type=F32)


def tn(a, b):
    return lax.dot_general(a, b, (((0,), (0,)), ((), ())), preferred_element_type=F32)


def kernel(
    enc_ref, w_ref, q_ref, cg_ref, ctx_ref, ge_ref,
    wb, w_st, enc_buf, enc_t, acc, q_v, cg_v, ctx_v, kv_v, gkv_v, xs, xr, ys, yr,
    loc, ring_s, ring_r, wy_s, wy_r, sib_s, sib_r, enc_s, enc_r, gx_s, gx_r, gy_s, gy_r,
):
    dp, pipe = lax.axis_index("dp"), lax.axis_index("pipe")
    core, z, row = dp % 2, (dp // 2) % NZ, dp // (2 * NZ)
    x, y = pipe // 4, pipe % 4
    dz = 1 - 2 * core
    orow = 1 - row

    def at_z(k):
        return (z + k * dz + 2 * NZ) % NZ

    def dp_of(r, zz, c):
        return {"dp": (r * NZ + zz) * 2 + c}

    def pipe_of(xx, yy):
        return {"pipe": xx * 4 + yy}

    far, near = dp_of(row, at_z(1), core), dp_of(row, at_z(-1), core)
    mate = dp_of(orow, z, core)
    twin = dp_of(row, z, 1 - core)
    xp, xm, xo = (x + 1) % 4, (x + 3) % 4, (x + 2) % 4
    yp, ym, yo = (y + 1) % 4, (y + 3) % 4, (y + 2) % 4
    x_up, x_dn = pipe_of(xp, y), pipe_of(xm, y)
    y_up, y_dn = pipe_of(x, yp), pipe_of(x, ym)

    started = []

    def send(src, dst, ss, rs, dev):
        c = pltpu.make_async_remote_copy(
            src_ref=src, dst_ref=dst, send_sem=ss, recv_sem=rs, device_id=dev, device_id_type=MESH
        )
        c.start()
        started.append(c)

    def arrived(dst, ss, rs, dev):
        pltpu.make_async_remote_copy(
            src_ref=dst, dst_ref=dst, send_sem=ss, recv_sem=rs, device_id=dev, device_id_type=MESH
        ).wait_recv()

    in_enc = pltpu.make_async_copy(enc_ref, enc_buf.at[:, pipe], loc.at[0])
    in_w = pltpu.make_async_copy(w_ref, w_st, loc.at[1])
    in_q = pltpu.make_async_copy(q_ref, q_v, loc.at[2])
    in_cg = pltpu.make_async_copy(cg_ref, cg_v, loc.at[3])
    in_enc.start()
    in_w.start()
    in_q.start()
    in_cg.start()

    barrier = pltpu.get_barrier_semaphore()
    for dev in (far, near, mate, twin, x_up, x_dn, y_up, y_dn):
        pl.semaphore_signal(barrier, inc=1, device_id=dev, device_id_type=MESH)
    pl.semaphore_wait(barrier, 8)

    groups = [("a", 0, 2), ("a", 2, 2), ("b", 4, 1), ("b", 5, 1), ("b", 6, 1), ("b", 7, 1)]

    def piece(g, zz):
        kind, h0, n = groups[g]
        if kind == "a":
            return wb.at[pl.ds(h0, n), core, row, zz]
        return wb.at[h0, core, :, zz]

    def rearrange(h):
        wb[h, core, row, z, :, :HD] = w_st[:, h * HD : (h + 1) * HD]
        wb[h, core, row, z, :, HD:] = w_st[:, (HEADS + h) * HD : (HEADS + h + 1) * HD]

    def mate_send(k, src):
        send(src, src, wy_s.at[k], wy_r.at[k], mate)

    def spread(g, k, zz):
        if g == 0:
            mate_send(k, wb.at[0, core, row, zz])
        if g == 5:
            p = piece(g, zz)
            send(p, p, sib_s.at[10 + k], sib_r.at[10 + k], twin)

    def far_step(g, k):
        p = piece(g, at_z(-k))
        if k >= 1:
            arrived(p, ring_s.at[g, k - 1], ring_r.at[g, k - 1], near)
        elif g < 2:
            for h in range(2 * g, 2 * g + 2):
                rearrange(h)
        if k <= 3:
            send(p, p, ring_s.at[g, k], ring_r.at[g, k], far)
        spread(g, k, at_z(-k))

    def near_step(g, k):
        p = piece(g, at_z(k))
        if k >= 1:
            arrived(p, ring_s.at[g, 3 + k], ring_r.at[g, 3 + k], far)
        if k <= 2:
            send(p, p, ring_s.at[g, 4 + k], ring_r.at[g, 4 + k], near)
        if k >= 1:
            spread(g, 4 + k, at_z(k))

    def group_end(g):
        kind, h0, n = groups[g]
        if g < 5:
            p = wb.at[pl.ds(h0, n), core, row] if kind == "a" else wb.at[h0, core]
            send(p, p, sib_s.at[g], sib_r.at[g], twin)

    def mate_bulk(h):
        mate_send(7 + h, wb.at[h, core, row])

    def mate_b():
        for h in range(4, 8):
            rearrange(h)
        mate_send(11, wb.at[pl.ds(4, 4), core, row, z])

    def mate_b_in():
        arrived(wb.at[pl.ds(4, 4), core, orow, z], wy_s.at[11], wy_r.at[11], mate)

    def mate_done(h):
        if h == 0:
            for i in range(8):
                zz = at_z(-i) if i <= 4 else at_z(i - 4)
                arrived(wb.at[0, core, orow, zz], wy_s.at[i], wy_r.at[i], mate)
        else:
            arrived(wb.at[h, core, orow], wy_s.at[7 + h], wy_r.at[7 + h], mate)
        p = wb.at[h, core, orow]
        send(p, p, sib_s.at[6 + h], sib_r.at[6 + h], twin)

    oc = 1 - core

    def twin_own(g):
        kind, h0, n = groups[g]
        if kind == "a":
            p = wb.at[pl.ds(h0, n), oc, row]
        else:
            p = wb.at[h0, oc]
        arrived(p, sib_s.at[g], sib_r.at[g], twin)

    def twin_done(h):
        if h < 4:
            arrived(wb.at[h, oc, orow], sib_s.at[6 + h], sib_r.at[6 + h], twin)
        elif h < 7:
            twin_own(h - 2)
        else:
            for k in range(8):
                zz = at_z(k) if k <= 4 else at_z(4 - k)
                arrived(wb.at[7, oc, :, zz], sib_s.at[10 + k], sib_r.at[10 + k], twin)

    def enc_x(yy, i):
        b = enc_buf.at[:, x * 4 + yy]
        send(b, b, enc_s.at[4 + i], enc_r.at[4 + i], x_up)
        send(b, b, enc_s.at[8 + i], enc_r.at[8 + i], x_dn)

    def enc_x2(yy, i):
        b = enc_buf.at[:, xm * 4 + yy]
        arrived(b, enc_s.at[4 + i], enc_r.at[4 + i], x_dn)
        b = b.at[0]
        send(b, b, enc_s.at[12 + i], enc_r.at[12 + i], x_up)
        b = enc_buf.at[:, xp * 4 + yy]
        arrived(b, enc_s.at[8 + i], enc_r.at[8 + i], x_up)
        b = b.at[1]
        send(b, b, enc_s.at[16 + i], enc_r.at[16 + i], x_dn)

    def enc_0():
        b = enc_buf.at[:, pipe]
        send(b, b, enc_s.at[0], enc_r.at[0], y_up)
        send(b, b, enc_s.at[1], enc_r.at[1], y_dn)
        enc_x(y, 0)

    def enc_1():
        b = enc_buf.at[:, x * 4 + ym]
        arrived(b, enc_s.at[0], enc_r.at[0], y_dn)
        b = b.at[0]
        send(b, b, enc_s.at[2], enc_r.at[2], y_up)
        b = enc_buf.at[:, x * 4 + yp]
        arrived(b, enc_s.at[1], enc_r.at[1], y_up)
        b = b.at[1]
        send(b, b, enc_s.at[3], enc_r.at[3], y_dn)
        enc_x(ym, 1)
        enc_x(yp, 2)

    def enc_2():
        arrived(enc_buf.at[0, x * 4 + yo], enc_s.at[2], enc_r.at[2], y_dn)
        arrived(enc_buf.at[1, x * 4 + yo], enc_s.at[3], enc_r.at[3], y_up)
        enc_x(yo, 3)

    def enc_end():
        for i, yy in enumerate((y, ym, yp, yo)):
            arrived(enc_buf.at[0, xo * 4 + yy], enc_s.at[12 + i], enc_r.at[12 + i], x_dn)
            arrived(enc_buf.at[1, xo * 4 + yy], enc_s.at[16 + i], enc_r.at[16 + i], x_up)

    def transpose(c):
        b = enc_buf[c // 2, (c % 2) * 8 : (c % 2) * 8 + 8]
        enc_t[:, c * 512 : (c + 1) * 512] = b.reshape(512, TOK).T

    def project(h):
        w = wb[h].reshape(WIDTH, 2 * HD)
        kv_v[...] = nn(enc_t[...], w).astype(BF16)

    def attend(h):
        cols = slice(h * HD, (h + 1) * HD)
        rows = [slice(i * SEQ, (i + 1) * SEQ) for i in range(TOK // SEQ)]
        k = [kv_v[r, :HD] for r in rows]
        v = [kv_v[r, HD:] for r in rows]
        q = [q_v[r, cols] for r in rows]
        cg = [cg_v[r, cols] for r in rows]
        s = [nt(a, b) for a, b in zip(k, q)]
        gp = [nt(a, b) for a, b in zip(v, cg)]
        e = [jnp.exp(t - jnp.max(t, axis=0, keepdims=True)) for t in s]
        p = [t * (1.0 / jnp.sum(t, axis=0, keepdims=True)) for t in e]
        pb = [t.astype(BF16) for t in p]
        gs = [(a * (b - jnp.sum(b * a, axis=0, keepdims=True))).astype(BF16) for a, b in zip(p, gp)]
        for i, r in enumerate(rows):
            gkv_v[r, :HD] = nn(gs[i], q[i]).astype(BF16)
            gkv_v[r, HD:] = nn(pb[i], cg[i]).astype(BF16)
        for i, r in enumerate(rows):
            ctx_v[r, cols] = tn(pb[i], v[i]).astype(BF16)

    def grad(h):
        g = gkv_v[...]
        for c in range(4):
            j, r = c // 2, c % 2
            t = nt(wb[h, j, r].reshape(512, 2 * HD), g).reshape(NZ, 64, TOK)
            acc[j, r] = t if first[0] else acc[j, r] + t
        first[0] = False

    first = [True]

    def own_start():
        in_enc.wait()
        enc_0()
        in_w.wait()

    def enc_hop(i):
        enc_x2((y, ym, yp, yo)[i], i)

    def enc_all():
        enc_end()
        in_q.wait()
        in_cg.wait()

    owned = set()

    def project_step(h):
        if h < 4 and h // 2 not in owned:
            owned.add(h // 2)
            twin_own(h // 2)
        twin_done(h)
        project(h)

    steps = {
        "e0": own_start, "e1": enc_1, "e2": enc_2, "ex": enc_hop, "ee": enc_all, "t": transpose,
        "yb": mate_b, "ybw": mate_b_in, "F": far_step, "N": near_step, "end": group_end,
        "ys": mate_bulk, "yd": mate_done, "P": project_step, "A": attend, "G": grad,
    }
    for name, *at in ORDER:
        steps[name](*at)

    out_ctx = pltpu.make_async_copy(ctx_v, ctx_ref, loc.at[4])
    out_ctx.start()
    g7 = gkv_v[...]
    order = (yo, yp, ym, y)

    def blocks(ref, j, xx):
        return ref.at[j, xx // 2, pl.ds((xx % 2) * 4, 4)]

    def last(j, xx):
        w = blocks(wb.at[7], j, xx)[...].reshape(TOK, 2 * HD)
        return blocks(acc, j, xx)[...] + nt(w, g7).reshape(4, 64, TOK)

    def one(j, xx, yy):
        return acc.at[j, xx // 2, (xx % 2) * 4 + yy]

    def gx(m, r):
        send(xs.at[m, order[r]], xr.at[m, order[r]], gx_s.at[m, r], gx_r.at[m, r], x_up if m % 2 == 0 else x_dn)

    def gx_in(m, r):
        dev = x_dn if m % 2 == 0 else x_up
        arrived(xr.at[m, order[r]], gx_s.at[m, r], gx_r.at[m, r], dev)
        return xr[m, order[r]].astype(F32)

    def relay(r):
        xs[4, order[r]] = (gx_in(0, r) + one(0, xp, order[r])[...]).astype(BF16)
        gx(4, r)
        xs[5, order[r]] = (gx_in(1, r) + one(1, xm, order[r])[...]).astype(BF16)
        gx(5, r)

    def pair(m, r):
        gx(m, r)
        gx(m + 1, r)

    xs[0] = last(0, xo).astype(BF16)
    xs[1] = last(1, xo).astype(BF16)
    pair(0, 0)
    pair(0, 1)
    xs[2] = last(1, xp).astype(BF16)
    xs[3] = last(0, xm).astype(BF16)
    pair(2, 0)
    pair(0, 2)
    blocks(acc, 0, xp)[...] = last(0, xp)
    blocks(acc, 1, xm)[...] = last(1, xm)
    relay(0)
    pair(0, 3)
    pair(2, 1)
    blocks(acc, 0, x)[...] = last(0, x)
    blocks(acc, 1, x)[...] = last(1, x)
    relay(1)
    pair(2, 2)
    relay(2)
    pair(2, 3)

    def total(r):
        t1 = one(1, x, order[r])[...] + gx_in(2, r)
        t0 = one(0, x, order[r])[...] + gx_in(3, r)
        return t0 + gx_in(4, r), t1 + gx_in(5, r)

    def gy(m, v):
        ys[m] = v.astype(BF16)
        send(ys.at[m], yr.at[m], gy_s.at[m], gy_r.at[m], y_up if m % 2 == 0 else y_dn)

    def gy_in(m):
        arrived(yr.at[m], gy_s.at[m], gy_r.at[m], y_dn if m % 2 == 0 else y_up)
        return yr[m].astype(F32)

    s0, s1 = total(0)
    gy(0, s0)
    gy(1, s1)
    relay(3)
    u0, u1 = total(1)
    gy(2, u1)
    d0, d1 = total(2)
    gy(3, d0)
    gy(4, u0 + gy_in(0))
    gy(5, d1 + gy_in(1))
    o0, o1 = total(3)
    ge_ref[0] = (o0 + gy_in(3) + gy_in(4)).astype(BF16)
    ge_ref[1] = (o1 + gy_in(2) + gy_in(5)).astype(BF16)

    for c in started:
        c.wait_send()
    out_ctx.wait()


def local(encoder_out, key_value_weight, queries, context_gradient):
    any_space = pl.BlockSpec(memory_space=pl.ANY)
    vmem = pl.BlockSpec(memory_space=pltpu.VMEM)
    dma = pltpu.SemaphoreType.DMA
    ctx, ge = pl.pallas_call(
        kernel,
        out_shape=(
            jax.ShapeDtypeStruct((TOK, HEADS * HD), BF16),
            jax.ShapeDtypeStruct((2, 64, TOK), BF16),
        ),
        in_specs=[any_space] * 4,
        out_specs=(any_space, vmem),
        scratch_shapes=[
            pltpu.VMEM((HEADS, 2, 2, NZ, 64, 2 * HD), BF16),
            pltpu.VMEM((64, WIDTH), BF16),
            pltpu.VMEM((2, 16, 64, TOK), BF16),
            pltpu.VMEM((TOK, WIDTH), BF16),
            pltpu.VMEM((2, 2, NZ, 64, TOK), F32),
            pltpu.VMEM((TOK, HEADS * HD), BF16),
            pltpu.VMEM((TOK, HEADS * HD), BF16),
            pltpu.VMEM((TOK, HEADS * HD), BF16),
            pltpu.VMEM((TOK, 2 * HD), BF16),
            pltpu.VMEM((TOK, 2 * HD), BF16),
            pltpu.VMEM((6, 4, 64, TOK), BF16),
            pltpu.VMEM((6, 4, 64, TOK), BF16),
            pltpu.VMEM((6, 64, TOK), BF16),
            pltpu.VMEM((6, 64, TOK), BF16),
            dma((5,)),
            dma((6, 7)),
            dma((6, 7)),
            dma((12,)),
            dma((12,)),
            dma((18,)),
            dma((18,)),
            dma((20,)),
            dma((20,)),
            dma((6, 4)),
            dma((6, 4)),
            dma((6,)),
            dma((6,)),
        ],
        compiler_params=pltpu.CompilerParams(
            collective_id=0, has_side_effects=True, vmem_limit_bytes=LIMIT * 1024 * 1024
        ),
    )(
        encoder_out.reshape(2, 64, TOK),
        key_value_weight[0],
        queries[0],
        context_gradient[0],
    )
    return ctx[None], ge.reshape(2 * 64, TOK)


def solution(mesh):
    return jax.shard_map(
        local,
        mesh=mesh,
        in_specs=(P("pipe", "dp"), P("pipe", "dp", None), P("pipe", "dp", None), P("pipe", "dp", None)),
        out_specs=(P("pipe", "dp", None), P("pipe", "dp")),
        check_vma=False,
    )
```

```python
import jax
import jax.numpy as jnp
from jax import lax
from jax.experimental import pallas as pl
from jax.experimental.pallas import tpu as pltpu
from jax.sharding import PartitionSpec as P

MESH = pl.DeviceIdType.MESH
HEADS = 8
HD = 128
SEQ = 128
TOK = 256
WIDTH = 2048
NZ = 8
PARTS = 4
LIMIT = 63488
F32 = jnp.float32
BF16 = jnp.bfloat16

ORDER = [
    ("e0",), ("yb",), ("F", 0, 0), ("N", 0, 0), ("F", 1, 0), ("N", 1, 0), ("F", 0, 1), ("ex", 0), ("N", 0, 1),
    ("F", 1, 1), ("N", 1, 1), ("e1",), ("F", 0, 2), ("N", 0, 2), ("F", 1, 2), ("ybw",), ("F", 2, 0),
    ("N", 2, 0), ("F", 3, 0), ("N", 1, 2), ("N", 3, 0), ("F", 0, 3), ("ex", 1), ("N", 0, 3), ("F", 4, 0),
    ("N", 4, 0), ("F", 1, 3), ("ex", 2), ("F", 2, 1), ("N", 2, 1), ("e2",), ("F", 3, 1), ("N", 1, 3),
    ("N", 3, 1), ("F", 0, 4), ("end", 0), ("ys", 1, 0), ("ys", 1, 1), ("F", 5, 0), ("N", 5, 0), ("F", 4, 1),
    ("ex", 3), ("N", 4, 1), ("F", 1, 4), ("end", 1), ("ys", 2, 0), ("ys", 2, 1), ("ys", 3, 0), ("ys", 3, 1),
    ("yd", 0, 0), ("F", 2, 2), ("N", 2, 2), ("ee",), ("t", 0), ("t", 1), ("F", 3, 2), ("t", 2), ("t", 3),
    ("N", 3, 2), ("yd", 1, 0), ("F", 5, 1), ("N", 5, 1), ("F", 4, 2), ("N", 4, 2), ("yd", 1, 1), ("F", 2, 3),
    ("N", 2, 3), ("F", 3, 3), ("P", 0, 1), ("N", 3, 3), ("A", 0, 1), ("F", 5, 2), ("yd", 2, 0), ("G", 0, 1),
    ("N", 5, 2), ("F", 4, 3), ("N", 4, 3), ("yd", 2, 1), ("F", 2, 4), ("end", 2), ("F", 3, 4), ("end", 3),
    ("F", 5, 3), ("N", 5, 3), ("P", 2, 4), ("F", 4, 4), ("end", 4), ("yd", 3, 0), ("A", 2, 4), ("G", 2, 4),
    ("F", 5, 4), ("end", 5), ("P", 5, 6), ("yd", 3, 1), ("A", 5, 6), ("G", 5, 6), ("P", 3, 7), ("A", 3, 7),
]


def nt(a, b):
    return lax.dot_general(a, b, (((1,), (1,)), ((), ())), preferred_element_type=F32)


def nn(a, b):
    return lax.dot_general(a, b, (((1,), (0,)), ((), ())), preferred_element_type=F32)


def tn(a, b):
    return lax.dot_general(a, b, (((0,), (0,)), ((), ())), preferred_element_type=F32)


def kernel(
    enc_ref, w_ref, q_ref, cg_ref, ctx_ref, ge_ref,
    wb, w_st, enc_buf, enc_t, acc, q_v, cg_v, ctx_v, kv_v, gkv_v, xs, xr, ys, yr,
    loc, ring_s, ring_r, wy_s, wy_r, sib_s, sib_r, enc_s, enc_r, gx_s, gx_r, gy_s, gy_r,
):
    dp, pipe = lax.axis_index("dp"), lax.axis_index("pipe")
    core, z, row = dp % 2, (dp // 2) % NZ, dp // (2 * NZ)
    x, y = pipe // 4, pipe % 4
    dz = 1 - 2 * core
    orow = 1 - row

    def at_z(k):
        return (z + k * dz + 2 * NZ) % NZ

    def dp_of(r, zz, c):
        return {"dp": (r * NZ + zz) * 2 + c}

    def pipe_of(xx, yy):
        return {"pipe": xx * 4 + yy}

    far, near = dp_of(row, at_z(1), core), dp_of(row, at_z(-1), core)
    mate = dp_of(orow, z, core)
    twin = dp_of(row, z, 1 - core)
    xp, xm, xo = (x + 1) % 4, (x + 3) % 4, (x + 2) % 4
    yp, ym, yo = (y + 1) % 4, (y + 3) % 4, (y + 2) % 4
    x_up, x_dn = pipe_of(xp, y), pipe_of(xm, y)
    y_up, y_dn = pipe_of(x, yp), pipe_of(x, ym)

    started = []

    def send(src, dst, ss, rs, dev):
        c = pltpu.make_async_remote_copy(
            src_ref=src, dst_ref=dst, send_sem=ss, recv_sem=rs, device_id=dev, device_id_type=MESH
        )
        c.start()
        started.append(c)

    def arrived(dst, ss, rs, dev):
        pltpu.make_async_remote_copy(
            src_ref=dst, dst_ref=dst, send_sem=ss, recv_sem=rs, device_id=dev, device_id_type=MESH
        ).wait_recv()

    in_enc = pltpu.make_async_copy(enc_ref, enc_buf.at[:, pipe], loc.at[0])
    in_w = pltpu.make_async_copy(w_ref, w_st, loc.at[1])
    in_q = pltpu.make_async_copy(q_ref, q_v, loc.at[2])
    in_cg = pltpu.make_async_copy(cg_ref, cg_v, loc.at[3])
    in_enc.start()
    in_w.start()
    in_q.start()
    in_cg.start()

    barrier = pltpu.get_barrier_semaphore()
    for dev in (far, near, mate, twin, x_up, x_dn, y_up, y_dn):
        pl.semaphore_signal(barrier, inc=1, device_id=dev, device_id_type=MESH)
    pl.semaphore_wait(barrier, 8)

    groups = [("a", 0, 2), ("a", 2, 2), ("b", 4, 1), ("b", 5, 1), ("b", 6, 1), ("b", 7, 1)]

    def piece(g, zz):
        kind, h0, n = groups[g]
        if kind == "a":
            return wb.at[pl.ds(h0, n), core, row, zz]
        return wb.at[h0, core, :, zz]

    def rearrange(h):
        wb[h, core, row, z, :, :HD] = w_st[:, h * HD : (h + 1) * HD]
        wb[h, core, row, z, :, HD:] = w_st[:, (HEADS + h) * HD : (HEADS + h + 1) * HD]

    def mate_send(k, src):
        send(src, src, wy_s.at[k], wy_r.at[k], mate)

    def spread(g, k, zz):
        if g == 0:
            mate_send(k, wb.at[0, core, row, zz])
        if g == 5:
            p = piece(g, zz)
            send(p, p, sib_s.at[10 + k], sib_r.at[10 + k], twin)

    def far_step(g, k):
        p = piece(g, at_z(-k))
        if k >= 1:
            arrived(p, ring_s.at[g, k - 1], ring_r.at[g, k - 1], near)
        elif g < 2:
            for h in range(2 * g, 2 * g + 2):
                rearrange(h)
        if k <= 3:
            send(p, p, ring_s.at[g, k], ring_r.at[g, k], far)
        spread(g, k, at_z(-k))

    def near_step(g, k):
        p = piece(g, at_z(k))
        if k >= 1:
            arrived(p, ring_s.at[g, 3 + k], ring_r.at[g, 3 + k], far)
        if k <= 2:
            send(p, p, ring_s.at[g, 4 + k], ring_r.at[g, 4 + k], near)
        if k >= 1:
            spread(g, 4 + k, at_z(k))

    def group_end(g):
        kind, h0, n = groups[g]
        if g < 5:
            p = wb.at[pl.ds(h0, n), core, row] if kind == "a" else wb.at[h0, core]
            send(p, p, sib_s.at[g], sib_r.at[g], twin)

    def mate_bulk(h, i):
        mate_send(6 + 2 * h + i, wb.at[h, core, row, pl.ds(4 * i, 4)])

    def mate_b():
        for h in range(4, 8):
            rearrange(h)
        mate_send(14, wb.at[pl.ds(4, 4), core, row, z])

    def mate_b_in():
        arrived(wb.at[pl.ds(4, 4), core, orow, z], wy_s.at[14], wy_r.at[14], mate)

    def mate_done(h, i):
        if h == 0:
            for j in range(8):
                zz = at_z(-j) if j <= 4 else at_z(j - 4)
                arrived(wb.at[0, core, orow, zz], wy_s.at[j], wy_r.at[j], mate)
            p = wb.at[0, core, orow]
        else:
            p = wb.at[h, core, orow, pl.ds(4 * i, 4)]
            arrived(p, wy_s.at[6 + 2 * h + i], wy_r.at[6 + 2 * h + i], mate)
        send(p, p, sib_s.at[18 + 2 * h + i], sib_r.at[18 + 2 * h + i], twin)

    oc = 1 - core

    def twin_own(g):
        kind, h0, n = groups[g]
        if kind == "a":
            p = wb.at[pl.ds(h0, n), oc, row]
        else:
            p = wb.at[h0, oc]
        arrived(p, sib_s.at[g], sib_r.at[g], twin)

    def twin_done(h):
        if h == 0:
            arrived(wb.at[0, oc, orow], sib_s.at[18], sib_r.at[18], twin)
        elif h < 4:
            for i in range(2):
                k = 18 + 2 * h + i
                arrived(wb.at[h, oc, orow, pl.ds(4 * i, 4)], sib_s.at[k], sib_r.at[k], twin)
        elif h < 7:
            twin_own(h - 2)
        else:
            for k in range(8):
                zz = at_z(k) if k <= 4 else at_z(4 - k)
                arrived(wb.at[7, oc, :, zz], sib_s.at[10 + k], sib_r.at[10 + k], twin)

    def enc_x(yy, i):
        b = enc_buf.at[:, x * 4 + yy]
        send(b, b, enc_s.at[4 + i], enc_r.at[4 + i], x_up)
        send(b, b, enc_s.at[8 + i], enc_r.at[8 + i], x_dn)

    def enc_x2(yy, i):
        b = enc_buf.at[:, xm * 4 + yy]
        arrived(b, enc_s.at[4 + i], enc_r.at[4 + i], x_dn)
        b = b.at[0]
        send(b, b, enc_s.at[12 + i], enc_r.at[12 + i], x_up)
        b = enc_buf.at[:, xp * 4 + yy]
        arrived(b, enc_s.at[8 + i], enc_r.at[8 + i], x_up)
        b = b.at[1]
        send(b, b, enc_s.at[16 + i], enc_r.at[16 + i], x_dn)

    def enc_0():
        b = enc_buf.at[:, pipe]
        send(b, b, enc_s.at[0], enc_r.at[0], y_up)
        send(b, b, enc_s.at[1], enc_r.at[1], y_dn)
        enc_x(y, 0)

    def enc_1():
        b = enc_buf.at[:, x * 4 + ym]
        arrived(b, enc_s.at[0], enc_r.at[0], y_dn)
        b = b.at[0]
        send(b, b, enc_s.at[2], enc_r.at[2], y_up)
        b = enc_buf.at[:, x * 4 + yp]
        arrived(b, enc_s.at[1], enc_r.at[1], y_up)
        b = b.at[1]
        send(b, b, enc_s.at[3], enc_r.at[3], y_dn)
        enc_x(ym, 1)
        enc_x(yp, 2)

    def enc_2():
        arrived(enc_buf.at[0, x * 4 + yo], enc_s.at[2], enc_r.at[2], y_dn)
        arrived(enc_buf.at[1, x * 4 + yo], enc_s.at[3], enc_r.at[3], y_up)
        enc_x(yo, 3)

    def enc_end():
        for i, yy in enumerate((y, ym, yp, yo)):
            arrived(enc_buf.at[0, xo * 4 + yy], enc_s.at[12 + i], enc_r.at[12 + i], x_dn)
            arrived(enc_buf.at[1, xo * 4 + yy], enc_s.at[16 + i], enc_r.at[16 + i], x_up)

    def transpose(c):
        b = enc_buf[c // 2, (c % 2) * 8 : (c % 2) * 8 + 8]
        enc_t[:, c * 512 : (c + 1) * 512] = b.reshape(512, TOK).T

    def project(hs):
        for n, h in enumerate(hs):
            kv_v[n] = nn(enc_t[...], wb[h].reshape(WIDTH, 2 * HD)).astype(BF16)

    def attend(*hs):
        at = [
            (n, slice(i * SEQ, (i + 1) * SEQ), slice(h * HD, (h + 1) * HD))
            for n, h in enumerate(hs)
            for i in range(TOK // SEQ)
        ]
        k = [kv_v[n, r, :HD] for n, r, _ in at]
        v = [kv_v[n, r, HD:] for n, r, _ in at]
        q = [q_v[r, c] for _, r, c in at]
        cg = [cg_v[r, c] for _, r, c in at]
        s = [nt(a, b) for a, b in zip(k, q)]
        gp = [nt(a, b) for a, b in zip(v, cg)]
        e = [jnp.exp(t - jnp.max(t, axis=0, keepdims=True)) for t in s]
        p = [t * (1.0 / jnp.sum(t, axis=0, keepdims=True)) for t in e]
        pb = [t.astype(BF16) for t in p]
        gs = [(a * (b - jnp.sum(b * a, axis=0, keepdims=True))).astype(BF16) for a, b in zip(p, gp)]
        for i, (n, r, c) in enumerate(at):
            gkv_v[n, r, :HD] = nn(gs[i], q[i]).astype(BF16)
            gkv_v[n, r, HD:] = nn(pb[i], cg[i]).astype(BF16)
        for i, (n, r, c) in enumerate(at):
            ctx_v[r, c] = tn(pb[i], v[i]).astype(BF16)

    def grad(*hs):
        for c in range(4):
            j, r = c // 2, c % 2
            t = sum(nt(wb[h, j, r].reshape(512, 2 * HD), gkv_v[n]) for n, h in enumerate(hs))
            t = t.reshape(NZ, 64, TOK)
            acc[j, r] = t if first[0] else acc[j, r] + t
        first[0] = False

    first = [True]

    def own_start():
        in_enc.wait()
        enc_0()
        in_w.wait()

    def enc_hop(i):
        enc_x2((y, ym, yp, yo)[i], i)

    def enc_all():
        enc_end()
        in_q.wait()
        in_cg.wait()

    owned = set()

    def project_step(*hs):
        for h in hs:
            if h < 4 and h // 2 not in owned:
                owned.add(h // 2)
                twin_own(h // 2)
            twin_done(h)
        project(hs)

    steps = {
        "e0": own_start, "e1": enc_1, "e2": enc_2, "ex": enc_hop, "ee": enc_all, "t": transpose,
        "yb": mate_b, "ybw": mate_b_in, "F": far_step, "N": near_step, "end": group_end,
        "ys": mate_bulk, "yd": mate_done, "P": project_step, "A": attend, "G": grad,
    }
    for name, *at in ORDER:
        steps[name](*at)

    out_ctx = pltpu.make_async_copy(ctx_v, ctx_ref, loc.at[4])
    out_ctx.start()
    final = [at for name, *at in ORDER if name == "P"][-1]
    g_last = [gkv_v[n] for n in range(len(final))]
    order = (yo, yp, ym, y)

    def blocks(ref, j, xx):
        return ref.at[j, xx // 2, pl.ds((xx % 2) * 4, 4)]

    def last(j, xx):
        t = sum(nt(blocks(wb.at[h], j, xx)[...].reshape(TOK, 2 * HD), g) for h, g in zip(final, g_last))
        return blocks(acc, j, xx)[...] + t.reshape(4, 64, TOK)

    def one(j, xx, yy):
        return acc.at[j, xx // 2, (xx % 2) * 4 + yy]

    def gx(m, r):
        send(xs.at[m, order[r]], xr.at[m, order[r]], gx_s.at[m, r], gx_r.at[m, r], x_up if m % 2 == 0 else x_dn)

    def gx_in(m, r):
        dev = x_dn if m % 2 == 0 else x_up
        arrived(xr.at[m, order[r]], gx_s.at[m, r], gx_r.at[m, r], dev)
        return xr[m, order[r]].astype(F32)

    def relay(r):
        xs[4, order[r]] = (gx_in(0, r) + one(0, xp, order[r])[...]).astype(BF16)
        gx(4, r)
        xs[5, order[r]] = (gx_in(1, r) + one(1, xm, order[r])[...]).astype(BF16)
        gx(5, r)

    def pair(m, r):
        gx(m, r)
        gx(m + 1, r)

    xs[0] = last(0, xo).astype(BF16)
    xs[1] = last(1, xo).astype(BF16)
    pair(0, 0)
    pair(0, 1)
    xs[2] = last(1, xp).astype(BF16)
    xs[3] = last(0, xm).astype(BF16)
    pair(2, 0)
    pair(0, 2)
    blocks(acc, 0, xp)[...] = last(0, xp)
    blocks(acc, 1, xm)[...] = last(1, xm)
    relay(0)
    pair(0, 3)
    pair(2, 1)
    blocks(acc, 0, x)[...] = last(0, x)
    blocks(acc, 1, x)[...] = last(1, x)
    relay(1)
    pair(2, 2)
    relay(2)
    pair(2, 3)

    def total(r):
        t1 = one(1, x, order[r])[...] + gx_in(2, r)
        t0 = one(0, x, order[r])[...] + gx_in(3, r)
        return t0 + gx_in(4, r), t1 + gx_in(5, r)

    def gy(m, i, v):
        half = pl.ds(32 * i, 32)
        ys[m, half] = v.astype(BF16)
        dev = y_up if m % 2 == 0 else y_dn
        send(ys.at[m, half], yr.at[m, half], gy_s.at[m, i], gy_r.at[m, i], dev)

    def gy_in(m, i):
        half = pl.ds(32 * i, 32)
        arrived(yr.at[m, half], gy_s.at[m, i], gy_r.at[m, i], y_dn if m % 2 == 0 else y_up)
        return yr[m, half].astype(F32)

    def part(v, i):
        return v[32 * i : 32 * i + 32]

    s0, s1 = total(0)
    for i in range(2):
        gy(0, i, part(s0, i))
        gy(1, i, part(s1, i))
    relay(3)
    u0, u1 = total(1)
    for i in range(2):
        gy(2, i, part(u1, i))
    d0, d1 = total(2)
    for i in range(2):
        gy(3, i, part(d0, i))
    while started:
        started.pop(0).wait_send()
    for i in range(2):
        gy(4, i, part(u0, i) + gy_in(0, i))
        gy(5, i, part(d1, i) + gy_in(1, i))
    o0, o1 = total(3)
    for i in range(2):
        half = slice(32 * i, 32 * i + 32)
        ge_ref[0, half] = (part(o0, i) + gy_in(3, i) + gy_in(4, i)).astype(BF16)
        ge_ref[1, half] = (part(o1, i) + gy_in(2, i) + gy_in(5, i)).astype(BF16)

    for c in started:
        c.wait_send()
    out_ctx.wait()


def hand_on(ctx_ref, ge_ref, ctx_out, ge_out, ctx_v, ge_v, sem_in, sem_out):
    rows = TOK // PARTS
    parts = [tuple(r.at[pl.ds(i * rows, rows)] for r in (ctx_ref, ctx_v, ctx_out)) for i in range(PARTS)]
    parts.append((ge_ref, ge_v, ge_out))
    there = [pltpu.make_async_copy(s, v, sem_in.at[i]) for i, (s, v, _) in enumerate(parts)]
    on = [pltpu.make_async_copy(v, d, sem_out.at[i]) for i, (_, v, d) in enumerate(parts)]
    for c in there:
        c.start()
    for a, b in zip(there, on):
        a.wait()
        b.start()
    for c in on:
        c.wait()


def local(encoder_out, key_value_weight, queries, context_gradient):
    any_space = pl.BlockSpec(memory_space=pl.ANY)
    vmem = pl.BlockSpec(memory_space=pltpu.VMEM)
    dma = pltpu.SemaphoreType.DMA
    ctx, ge = pl.pallas_call(
        kernel,
        out_shape=(
            jax.ShapeDtypeStruct((TOK, HEADS * HD), BF16),
            jax.ShapeDtypeStruct((2, 64, TOK), BF16),
        ),
        in_specs=[any_space] * 4,
        out_specs=(any_space, vmem),
        scratch_shapes=[
            pltpu.VMEM((HEADS, 2, 2, NZ, 64, 2 * HD), BF16),
            pltpu.VMEM((64, WIDTH), BF16),
            pltpu.VMEM((2, 16, 64, TOK), BF16),
            pltpu.VMEM((TOK, WIDTH), BF16),
            pltpu.VMEM((2, 2, NZ, 64, TOK), F32),
            pltpu.VMEM((TOK, HEADS * HD), BF16),
            pltpu.VMEM((TOK, HEADS * HD), BF16),
            pltpu.VMEM((TOK, HEADS * HD), BF16),
            pltpu.VMEM((2, TOK, 2 * HD), BF16),
            pltpu.VMEM((2, TOK, 2 * HD), BF16),
            pltpu.VMEM((6, 4, 64, TOK), BF16),
            pltpu.VMEM((6, 4, 64, TOK), BF16),
            pltpu.VMEM((6, 64, TOK), BF16),
            pltpu.VMEM((6, 64, TOK), BF16),
            dma((5,)),
            dma((6, 7)),
            dma((6, 7)),
            dma((15,)),
            dma((15,)),
            dma((26,)),
            dma((26,)),
            dma((20,)),
            dma((20,)),
            dma((6, 4)),
            dma((6, 4)),
            dma((6, 2)),
            dma((6, 2)),
        ],
        compiler_params=pltpu.CompilerParams(
            collective_id=0, has_side_effects=True, vmem_limit_bytes=LIMIT * 1024
        ),
    )(
        encoder_out.reshape(2, 64, TOK),
        key_value_weight[0],
        queries[0],
        context_gradient[0],
    )
    ctx, ge = pl.pallas_call(
        hand_on,
        out_shape=(
            jax.ShapeDtypeStruct((TOK, HEADS * HD), BF16),
            jax.ShapeDtypeStruct((2, 64, TOK), BF16),
        ),
        in_specs=[any_space] * 2,
        out_specs=(any_space, any_space),
        scratch_shapes=[
            pltpu.VMEM((TOK, HEADS * HD), BF16),
            pltpu.VMEM((2, 64, TOK), BF16),
            dma((PARTS + 1,)),
            dma((PARTS + 1,)),
        ],
        compiler_params=pltpu.CompilerParams(vmem_limit_bytes=LIMIT * 1024),
    )(ctx, ge)
    return ctx[None], ge.reshape(2 * 64, TOK)


def solution(mesh):
    return jax.shard_map(
        local,
        mesh=mesh,
        in_specs=(P("pipe", "dp"), P("pipe", "dp", None), P("pipe", "dp", None), P("pipe", "dp", None)),
        out_specs=(P("pipe", "dp", None), P("pipe", "dp")),
        check_vma=False,
    )
```

```python
import jax
import jax.numpy as jnp
from jax import lax
from jax.experimental import pallas as pl
from jax.experimental.pallas import tpu as pltpu
from jax.sharding import PartitionSpec as P

MESH = pl.DeviceIdType.MESH
HEADS = 8
HD = 128
SEQ = 128
TOK = 256
WIDTH = 2048
NZ = 8
KEEP = 16
PARTS = 4
LIMIT = 63488
F32 = jnp.float32
BF16 = jnp.bfloat16

ORDER = [
    ("e0",), ("yb",), ("F", 0, 0), ("N", 0, 0), ("F", 1, 0), ("N", 1, 0), ("F", 0, 1), ("ex", 0), ("N", 0, 1),
    ("F", 1, 1), ("N", 1, 1), ("e1",), ("F", 0, 2), ("N", 0, 2), ("F", 1, 2), ("ybw",), ("F", 2, 0),
    ("N", 2, 0), ("F", 3, 0), ("N", 3, 0), ("N", 1, 2), ("ex", 1), ("F", 0, 3), ("N", 0, 3), ("F", 4, 0),
    ("N", 4, 0), ("ex", 2), ("F", 1, 3), ("F", 2, 1), ("N", 2, 1), ("F", 3, 1), ("N", 3, 1), ("e2",),
    ("N", 1, 3), ("F", 0, 4), ("F", 5, 0), ("N", 5, 0), ("end", 0), ("F", 4, 1), ("N", 4, 1), ("F", 1, 4),
    ("end", 1), ("ys", 2, 0), ("ys", 2, 1), ("ys", 3, 0), ("ex", 3), ("F", 2, 2), ("ys", 3, 1), ("N", 2, 2),
    ("F", 3, 2), ("N", 3, 2), ("yd", 0, 0), ("F", 5, 1), ("ee",), ("t", 0), ("t", 1), ("N", 5, 1), ("t", 2),
    ("t", 3), ("F", 4, 2), ("P", 0, 1), ("N", 4, 2), ("yd", 2, 0), ("F", 2, 3), ("A", 0, 1), ("N", 2, 3),
    ("G", 0, 1), ("F", 3, 3), ("N", 3, 3), ("yd", 2, 1), ("F", 5, 2), ("N", 5, 2), ("F", 4, 3), ("N", 4, 3),
    ("yd", 3, 0), ("F", 2, 4), ("end", 2), ("F", 3, 4), ("end", 3), ("F", 5, 3), ("N", 5, 3), ("P", 2, 4),
    ("F", 4, 4), ("end", 4), ("yd", 3, 1), ("A", 2, 4), ("G", 2, 4), ("F", 5, 4), ("end", 5), ("P", 5, 6),
    ("A", 5, 6), ("G", 5, 6), ("P", 3, 7), ("A", 3, 7),
]


def nt(a, b):
    return lax.dot_general(a, b, (((1,), (1,)), ((), ())), preferred_element_type=F32)


def nn(a, b):
    return lax.dot_general(a, b, (((1,), (0,)), ((), ())), preferred_element_type=F32)


def tn(a, b):
    return lax.dot_general(a, b, (((0,), (0,)), ((), ())), preferred_element_type=F32)


def kernel(
    enc_ref, w_ref, q_ref, cg_ref, ctx_ref, ge_ref,
    wb, w_st, enc_buf, enc_t, acc, q_v, cg_v, ctx_v, kv_v, gkv_v, xs, xr, ys, yr,
    loc, ring_s, ring_r, wy_s, wy_r, sib_s, sib_r, enc_s, enc_r, gx_s, gx_r, gy_s, gy_r,
):
    dp, pipe = lax.axis_index("dp"), lax.axis_index("pipe")
    core, z, row = dp % 2, (dp // 2) % NZ, dp // (2 * NZ)
    x, y = pipe // 4, pipe % 4
    dz = 1 - 2 * core
    orow = 1 - row

    def at_z(k):
        return (z + k * dz + 2 * NZ) % NZ

    def dp_of(r, zz, c):
        return {"dp": (r * NZ + zz) * 2 + c}

    def pipe_of(xx, yy):
        return {"pipe": xx * 4 + yy}

    far, near = dp_of(row, at_z(1), core), dp_of(row, at_z(-1), core)
    mate = dp_of(orow, z, core)
    twin = dp_of(row, z, 1 - core)
    xp, xm, xo = (x + 1) % 4, (x + 3) % 4, (x + 2) % 4
    yp, ym, yo = (y + 1) % 4, (y + 3) % 4, (y + 2) % 4
    x_up, x_dn = pipe_of(xp, y), pipe_of(xm, y)
    y_up, y_dn = pipe_of(x, yp), pipe_of(x, ym)

    started = []

    def send(src, dst, ss, rs, dev):
        c = pltpu.make_async_remote_copy(
            src_ref=src, dst_ref=dst, send_sem=ss, recv_sem=rs, device_id=dev, device_id_type=MESH
        )
        c.start()
        started.append(c)

    def sent(keep):
        while len(started) > keep:
            started.pop(0).wait_send()

    def arrived(dst, ss, rs, dev):
        pltpu.make_async_remote_copy(
            src_ref=dst, dst_ref=dst, send_sem=ss, recv_sem=rs, device_id=dev, device_id_type=MESH
        ).wait_recv()

    in_enc = pltpu.make_async_copy(enc_ref, enc_buf.at[:, pipe], loc.at[0])
    in_w = pltpu.make_async_copy(w_ref, w_st, loc.at[1])
    in_q = pltpu.make_async_copy(q_ref, q_v, loc.at[2])
    in_cg = pltpu.make_async_copy(cg_ref, cg_v, loc.at[3])
    in_enc.start()
    in_w.start()
    in_q.start()
    in_cg.start()

    barrier = pltpu.get_barrier_semaphore()
    for dev in (far, near, mate, twin, x_up, x_dn, y_up, y_dn):
        pl.semaphore_signal(barrier, inc=1, device_id=dev, device_id_type=MESH)
    pl.semaphore_wait(barrier, 8)

    groups = [("a", 0, 2), ("a", 2, 2), ("b", 4, 1), ("b", 5, 1), ("b", 6, 1), ("b", 7, 1)]

    def piece(g, zz):
        kind, h0, n = groups[g]
        if kind == "a":
            return wb.at[pl.ds(h0, n), core, row, zz]
        return wb.at[h0, core, :, zz]

    def rearrange(h):
        wb[h, core, row, z, :, :HD] = w_st[:, h * HD : (h + 1) * HD]
        wb[h, core, row, z, :, HD:] = w_st[:, (HEADS + h) * HD : (HEADS + h + 1) * HD]

    def mate_send(k, src):
        send(src, src, wy_s.at[k], wy_r.at[k], mate)

    def spread(g, k, zz):
        if g == 0:
            mate_send(k, piece(0, zz))
        if g == 5:
            p = piece(g, zz)
            send(p, p, sib_s.at[10 + k], sib_r.at[10 + k], twin)

    def far_step(g, k):
        p = piece(g, at_z(-k))
        if k >= 1:
            arrived(p, ring_s.at[g, k - 1], ring_r.at[g, k - 1], near)
        elif g < 2:
            for h in range(2 * g, 2 * g + 2):
                rearrange(h)
        if k <= 3:
            send(p, p, ring_s.at[g, k], ring_r.at[g, k], far)
        spread(g, k, at_z(-k))

    def near_step(g, k):
        p = piece(g, at_z(k))
        if k >= 1:
            arrived(p, ring_s.at[g, 3 + k], ring_r.at[g, 3 + k], far)
        if k <= 2:
            send(p, p, ring_s.at[g, 4 + k], ring_r.at[g, 4 + k], near)
        if k >= 1:
            spread(g, 4 + k, at_z(k))

    def group_end(g):
        kind, h0, n = groups[g]
        if g < 5:
            p = wb.at[pl.ds(h0, n), core, row] if kind == "a" else wb.at[h0, core]
            send(p, p, sib_s.at[g], sib_r.at[g], twin)

    def mate_bulk(h, i):
        mate_send(6 + 2 * h + i, wb.at[h, core, row, pl.ds(4 * i, 4)])

    def mate_b():
        for h in range(4, 8):
            rearrange(h)
        mate_send(14, wb.at[pl.ds(4, 4), core, row, z])

    def mate_b_in():
        arrived(wb.at[pl.ds(4, 4), core, orow, z], wy_s.at[14], wy_r.at[14], mate)

    def mate_done(h, i):
        if h == 0:
            for j in range(8):
                zz = at_z(-j) if j <= 4 else at_z(j - 4)
                arrived(wb.at[pl.ds(0, 2), core, orow, zz], wy_s.at[j], wy_r.at[j], mate)
            p = wb.at[pl.ds(0, 2), core, orow]
        else:
            p = wb.at[h, core, orow, pl.ds(4 * i, 4)]
            arrived(p, wy_s.at[6 + 2 * h + i], wy_r.at[6 + 2 * h + i], mate)
        send(p, p, sib_s.at[18 + 2 * h + i], sib_r.at[18 + 2 * h + i], twin)

    oc = 1 - core

    def twin_own(g):
        kind, h0, n = groups[g]
        if kind == "a":
            p = wb.at[pl.ds(h0, n), oc, row]
        else:
            p = wb.at[h0, oc]
        arrived(p, sib_s.at[g], sib_r.at[g], twin)

    def twin_done(h):
        if h < 2:
            if "pair" not in owned:
                owned.add("pair")
                arrived(wb.at[pl.ds(0, 2), oc, orow], sib_s.at[18], sib_r.at[18], twin)
        elif h < 4:
            for i in range(2):
                k = 18 + 2 * h + i
                arrived(wb.at[h, oc, orow, pl.ds(4 * i, 4)], sib_s.at[k], sib_r.at[k], twin)
        elif h < 7:
            twin_own(h - 2)
        else:
            for k in range(8):
                zz = at_z(k) if k <= 4 else at_z(4 - k)
                arrived(wb.at[7, oc, :, zz], sib_s.at[10 + k], sib_r.at[10 + k], twin)

    def enc_x(yy, i):
        b = enc_buf.at[:, x * 4 + yy]
        send(b, b, enc_s.at[4 + i], enc_r.at[4 + i], x_up)
        send(b, b, enc_s.at[8 + i], enc_r.at[8 + i], x_dn)

    def enc_x2(yy, i):
        b = enc_buf.at[:, xm * 4 + yy]
        arrived(b, enc_s.at[4 + i], enc_r.at[4 + i], x_dn)
        b = b.at[0]
        send(b, b, enc_s.at[12 + i], enc_r.at[12 + i], x_up)
        b = enc_buf.at[:, xp * 4 + yy]
        arrived(b, enc_s.at[8 + i], enc_r.at[8 + i], x_up)
        b = b.at[1]
        send(b, b, enc_s.at[16 + i], enc_r.at[16 + i], x_dn)

    def enc_0():
        b = enc_buf.at[:, pipe]
        send(b, b, enc_s.at[0], enc_r.at[0], y_up)
        send(b, b, enc_s.at[1], enc_r.at[1], y_dn)
        enc_x(y, 0)

    def enc_1():
        b = enc_buf.at[:, x * 4 + ym]
        arrived(b, enc_s.at[0], enc_r.at[0], y_dn)
        b = b.at[0]
        send(b, b, enc_s.at[2], enc_r.at[2], y_up)
        b = enc_buf.at[:, x * 4 + yp]
        arrived(b, enc_s.at[1], enc_r.at[1], y_up)
        b = b.at[1]
        send(b, b, enc_s.at[3], enc_r.at[3], y_dn)
        enc_x(ym, 1)
        enc_x(yp, 2)

    def enc_2():
        arrived(enc_buf.at[0, x * 4 + yo], enc_s.at[2], enc_r.at[2], y_dn)
        arrived(enc_buf.at[1, x * 4 + yo], enc_s.at[3], enc_r.at[3], y_up)
        enc_x(yo, 3)

    def enc_end():
        for i, yy in enumerate((y, ym, yp, yo)):
            arrived(enc_buf.at[0, xo * 4 + yy], enc_s.at[12 + i], enc_r.at[12 + i], x_dn)
            arrived(enc_buf.at[1, xo * 4 + yy], enc_s.at[16 + i], enc_r.at[16 + i], x_up)

    def transpose(c):
        b = enc_buf[c // 2, (c % 2) * 8 : (c % 2) * 8 + 8]
        enc_t[:, c * 512 : (c + 1) * 512] = b.reshape(512, TOK).T

    def project(hs):
        for n, h in enumerate(hs):
            kv_v[n] = nn(enc_t[...], wb[h].reshape(WIDTH, 2 * HD)).astype(BF16)

    def attend(*hs):
        at = [
            (n, slice(i * SEQ, (i + 1) * SEQ), slice(h * HD, (h + 1) * HD))
            for n, h in enumerate(hs)
            for i in range(TOK // SEQ)
        ]
        k = [kv_v[n, r, :HD] for n, r, _ in at]
        v = [kv_v[n, r, HD:] for n, r, _ in at]
        q = [q_v[r, c] for _, r, c in at]
        cg = [cg_v[r, c] for _, r, c in at]
        s = [nt(a, b) for a, b in zip(k, q)]
        gp = [nt(a, b) for a, b in zip(v, cg)]
        e = [jnp.exp(t - jnp.max(t, axis=0, keepdims=True)) for t in s]
        p = [t * (1.0 / jnp.sum(t, axis=0, keepdims=True)) for t in e]
        pb = [t.astype(BF16) for t in p]
        gs = [(a * (b - jnp.sum(b * a, axis=0, keepdims=True))).astype(BF16) for a, b in zip(p, gp)]
        for i, (n, r, c) in enumerate(at):
            gkv_v[n, r, :HD] = nn(gs[i], q[i]).astype(BF16)
            gkv_v[n, r, HD:] = nn(pb[i], cg[i]).astype(BF16)
        for i, (n, r, c) in enumerate(at):
            ctx_v[r, c] = tn(pb[i], v[i]).astype(BF16)

    def grad(*hs):
        for c in range(4):
            j, r = c // 2, c % 2
            t = sum(nt(wb[h, j, r].reshape(512, 2 * HD), gkv_v[n]) for n, h in enumerate(hs))
            t = t.reshape(NZ, 64, TOK)
            acc[j, r] = t if first[0] else acc[j, r] + t
        first[0] = False

    first = [True]

    def own_start():
        in_enc.wait()
        enc_0()
        in_w.wait()

    def enc_hop(i):
        enc_x2((y, ym, yp, yo)[i], i)

    def enc_all():
        enc_end()
        in_q.wait()
        in_cg.wait()

    owned = set()

    def project_step(*hs):
        for h in hs:
            if h < 4 and h // 2 not in owned:
                owned.add(h // 2)
                twin_own(h // 2)
            twin_done(h)
        project(hs)

    steps = {
        "e0": own_start, "e1": enc_1, "e2": enc_2, "ex": enc_hop, "ee": enc_all, "t": transpose,
        "yb": mate_b, "ybw": mate_b_in, "F": far_step, "N": near_step, "end": group_end,
        "ys": mate_bulk, "yd": mate_done, "P": project_step, "A": attend, "G": grad,
    }
    for name, *at in ORDER:
        if name == "P":
            sent(KEEP)
        steps[name](*at)

    out_ctx = pltpu.make_async_copy(ctx_v, ctx_ref, loc.at[4])
    out_ctx.start()
    final = [at for name, *at in ORDER if name == "P"][-1]
    g_last = [gkv_v[n] for n in range(len(final))]
    order = (yo, yp, ym, y)

    def blocks(ref, j, xx):
        return ref.at[j, xx // 2, pl.ds((xx % 2) * 4, 4)]

    def last(j, xx):
        t = sum(nt(blocks(wb.at[h], j, xx)[...].reshape(TOK, 2 * HD), g) for h, g in zip(final, g_last))
        return blocks(acc, j, xx)[...] + t.reshape(4, 64, TOK)

    def one(j, xx, yy):
        return acc.at[j, xx // 2, (xx % 2) * 4 + yy]

    def gx(m, r):
        send(xs.at[m, order[r]], xr.at[m, order[r]], gx_s.at[m, r], gx_r.at[m, r], x_up if m % 2 == 0 else x_dn)

    def gx_in(m, r):
        dev = x_dn if m % 2 == 0 else x_up
        arrived(xr.at[m, order[r]], gx_s.at[m, r], gx_r.at[m, r], dev)
        return xr[m, order[r]].astype(F32)

    def relay(r):
        xs[4, order[r]] = (gx_in(0, r) + one(0, xp, order[r])[...]).astype(BF16)
        gx(4, r)
        xs[5, order[r]] = (gx_in(1, r) + one(1, xm, order[r])[...]).astype(BF16)
        gx(5, r)

    def pair(m, r):
        gx(m, r)
        gx(m + 1, r)

    xs[0] = last(0, xo).astype(BF16)
    xs[1] = last(1, xo).astype(BF16)
    pair(0, 0)
    pair(0, 1)
    xs[2] = last(1, xp).astype(BF16)
    xs[3] = last(0, xm).astype(BF16)
    pair(2, 0)
    pair(0, 2)
    sent(8)
    blocks(acc, 0, xp)[...] = last(0, xp)
    blocks(acc, 1, xm)[...] = last(1, xm)
    relay(0)
    pair(0, 3)
    pair(2, 1)
    blocks(acc, 0, x)[...] = last(0, x)
    blocks(acc, 1, x)[...] = last(1, x)
    relay(1)
    pair(2, 2)
    relay(2)
    pair(2, 3)

    def total(r):
        t1 = one(1, x, order[r])[...] + gx_in(2, r)
        t0 = one(0, x, order[r])[...] + gx_in(3, r)
        return t0 + gx_in(4, r), t1 + gx_in(5, r)

    def gy(m, i, v):
        half = pl.ds(32 * i, 32)
        ys[m, half] = v.astype(BF16)
        dev = y_up if m % 2 == 0 else y_dn
        send(ys.at[m, half], yr.at[m, half], gy_s.at[m, i], gy_r.at[m, i], dev)

    def gy_in(m, i):
        half = pl.ds(32 * i, 32)
        arrived(yr.at[m, half], gy_s.at[m, i], gy_r.at[m, i], y_dn if m % 2 == 0 else y_up)
        return yr[m, half].astype(F32)

    def part(v, i):
        return v[32 * i : 32 * i + 32]

    s0, s1 = total(0)
    for i in range(2):
        gy(0, i, part(s0, i))
        gy(1, i, part(s1, i))
    relay(3)
    u0, u1 = total(1)
    for i in range(2):
        gy(2, i, part(u1, i))
    d0, d1 = total(2)
    for i in range(2):
        gy(3, i, part(d0, i))
    for i in range(2):
        gy(4, i, part(u0, i) + gy_in(0, i))
        gy(5, i, part(d1, i) + gy_in(1, i))
    o0, o1 = total(3)
    for i in range(2):
        half = slice(32 * i, 32 * i + 32)
        ge_ref[0, half] = (part(o0, i) + gy_in(3, i) + gy_in(4, i)).astype(BF16)
        ge_ref[1, half] = (part(o1, i) + gy_in(2, i) + gy_in(5, i)).astype(BF16)

    sent(0)
    out_ctx.wait()


def hand_on(ctx_ref, ge_ref, ctx_out, ge_out, ctx_v, ge_v, sem_in, sem_out):
    rows = TOK // PARTS
    parts = [tuple(r.at[pl.ds(i * rows, rows)] for r in (ctx_ref, ctx_v, ctx_out)) for i in range(PARTS)]
    parts.append((ge_ref, ge_v, ge_out))
    there = [pltpu.make_async_copy(s, v, sem_in.at[i]) for i, (s, v, _) in enumerate(parts)]
    on = [pltpu.make_async_copy(v, d, sem_out.at[i]) for i, (_, v, d) in enumerate(parts)]
    for c in there:
        c.start()
    for a, b in zip(there, on):
        a.wait()
        b.start()
    for c in on:
        c.wait()


def local(encoder_out, key_value_weight, queries, context_gradient):
    any_space = pl.BlockSpec(memory_space=pl.ANY)
    vmem = pl.BlockSpec(memory_space=pltpu.VMEM)
    dma = pltpu.SemaphoreType.DMA
    ctx, ge = pl.pallas_call(
        kernel,
        out_shape=(
            jax.ShapeDtypeStruct((TOK, HEADS * HD), BF16),
            jax.ShapeDtypeStruct((2, 64, TOK), BF16),
        ),
        in_specs=[any_space] * 4,
        out_specs=(any_space, vmem),
        scratch_shapes=[
            pltpu.VMEM((HEADS, 2, 2, NZ, 64, 2 * HD), BF16),
            pltpu.VMEM((64, WIDTH), BF16),
            pltpu.VMEM((2, 16, 64, TOK), BF16),
            pltpu.VMEM((TOK, WIDTH), BF16),
            pltpu.VMEM((2, 2, NZ, 64, TOK), F32),
            pltpu.VMEM((TOK, HEADS * HD), BF16),
            pltpu.VMEM((TOK, HEADS * HD), BF16),
            pltpu.VMEM((TOK, HEADS * HD), BF16),
            pltpu.VMEM((2, TOK, 2 * HD), BF16),
            pltpu.VMEM((2, TOK, 2 * HD), BF16),
            pltpu.VMEM((6, 4, 64, TOK), BF16),
            pltpu.VMEM((6, 4, 64, TOK), BF16),
            pltpu.VMEM((6, 64, TOK), BF16),
            pltpu.VMEM((6, 64, TOK), BF16),
            dma((5,)),
            dma((6, 7)),
            dma((6, 7)),
            dma((15,)),
            dma((15,)),
            dma((26,)),
            dma((26,)),
            dma((20,)),
            dma((20,)),
            dma((6, 4)),
            dma((6, 4)),
            dma((6, 2)),
            dma((6, 2)),
        ],
        compiler_params=pltpu.CompilerParams(
            collective_id=0, has_side_effects=True, vmem_limit_bytes=LIMIT * 1024
        ),
    )(
        encoder_out.reshape(2, 64, TOK),
        key_value_weight[0],
        queries[0],
        context_gradient[0],
    )
    ctx, ge = pl.pallas_call(
        hand_on,
        out_shape=(
            jax.ShapeDtypeStruct((TOK, HEADS * HD), BF16),
            jax.ShapeDtypeStruct((2, 64, TOK), BF16),
        ),
        in_specs=[any_space] * 2,
        out_specs=(any_space, any_space),
        scratch_shapes=[
            pltpu.VMEM((TOK, HEADS * HD), BF16),
            pltpu.VMEM((2, 64, TOK), BF16),
            dma((PARTS + 1,)),
            dma((PARTS + 1,)),
        ],
        compiler_params=pltpu.CompilerParams(vmem_limit_bytes=LIMIT * 1024),
    )(ctx, ge)
    return ctx[None], ge.reshape(2 * 64, TOK)


def solution(mesh):
    return jax.shard_map(
        local,
        mesh=mesh,
        in_specs=(P("pipe", "dp"), P("pipe", "dp", None), P("pipe", "dp", None), P("pipe", "dp", None)),
        out_specs=(P("pipe", "dp", None), P("pipe", "dp")),
        check_vma=False,
    )
```

```python
import jax
import jax.numpy as jnp
from jax import lax
from jax.experimental import pallas as pl
from jax.experimental.pallas import tpu as pltpu
from jax.sharding import PartitionSpec as P

MESH = pl.DeviceIdType.MESH
HEADS = 8
HD = 128
SEQ = 128
TOK = 256
WIDTH = 2048
NZ = 8
KEEP = 16
PARTS = 4
LIMIT = 63488
F32 = jnp.float32
BF16 = jnp.bfloat16

ORDER = [
    ("e0",), ("yb",), ("F", 0, 0), ("N", 0, 0), ("F", 1, 0), ("N", 1, 0), ("F", 0, 1), ("ex", 0), ("N", 0, 1),
    ("F", 1, 1), ("N", 1, 1), ("e1",), ("F", 0, 2), ("N", 0, 2), ("F", 1, 2), ("ybw",), ("F", 2, 0),
    ("N", 2, 0), ("F", 3, 0), ("N", 3, 0), ("N", 1, 2), ("ex", 1), ("F", 0, 3), ("N", 0, 3), ("F", 4, 0),
    ("N", 4, 0), ("ex", 2), ("F", 1, 3), ("F", 2, 1), ("N", 2, 1), ("F", 3, 1), ("N", 3, 1), ("e2",),
    ("N", 1, 3), ("F", 0, 4), ("F", 5, 0), ("N", 5, 0), ("end", 0), ("F", 4, 1), ("N", 4, 1), ("F", 1, 4),
    ("end", 1), ("ys", 2, 0), ("ys", 2, 1), ("ys", 3, 0), ("ex", 3), ("F", 2, 2), ("ys", 3, 1), ("N", 2, 2),
    ("F", 3, 2), ("N", 3, 2), ("yd", 0, 0), ("F", 5, 1), ("ee",), ("t", 0), ("t", 1), ("N", 5, 1), ("t", 2),
    ("t", 3), ("F", 4, 2), ("P", 0, 1), ("N", 4, 2), ("yd", 2, 0), ("F", 2, 3), ("A", 0, 1), ("N", 2, 3),
    ("G", 0, 1), ("F", 3, 3), ("N", 3, 3), ("yd", 2, 1), ("F", 5, 2), ("N", 5, 2), ("F", 4, 3), ("N", 4, 3),
    ("yd", 3, 0), ("F", 2, 4), ("end", 2), ("F", 3, 4), ("end", 3), ("F", 5, 3), ("N", 5, 3), ("P", 2, 4),
    ("F", 4, 4), ("end", 4), ("yd", 3, 1), ("A", 2, 4), ("G", 2, 4), ("F", 5, 4), ("end", 5), ("P", 5, 6),
    ("A", 5, 6), ("G", 5, 6), ("P", 3, 7), ("A", 3, 7),
]


def nt(a, b):
    return lax.dot_general(a, b, (((1,), (1,)), ((), ())), preferred_element_type=F32)


def nn(a, b):
    return lax.dot_general(a, b, (((1,), (0,)), ((), ())), preferred_element_type=F32)


def tn(a, b):
    return lax.dot_general(a, b, (((0,), (0,)), ((), ())), preferred_element_type=F32)


def kernel(
    enc_ref, w_ref, q_ref, cg_ref, ctx_ref, ge_ref,
    wb, w_st, enc_buf, enc_t, acc, q_v, cg_v, ctx_v, kv_v, gkv_v, xs, xr, ys, yr,
    loc, ring_s, ring_r, wy_s, wy_r, sib_s, sib_r, enc_s, enc_r, gx_s, gx_r, gy_s, gy_r,
):
    dp, pipe = lax.axis_index("dp"), lax.axis_index("pipe")
    core, z, row = dp % 2, (dp // 2) % NZ, dp // (2 * NZ)
    x, y = pipe // 4, pipe % 4
    dz = 1 - 2 * core
    orow = 1 - row

    def at_z(k):
        return (z + k * dz + 2 * NZ) % NZ

    def dp_of(r, zz, c):
        return {"dp": (r * NZ + zz) * 2 + c}

    def pipe_of(xx, yy):
        return {"pipe": xx * 4 + yy}

    far, near = dp_of(row, at_z(1), core), dp_of(row, at_z(-1), core)
    mate = dp_of(orow, z, core)
    twin = dp_of(row, z, 1 - core)
    xp, xm, xo = (x + 1) % 4, (x + 3) % 4, (x + 2) % 4
    yp, ym, yo = (y + 1) % 4, (y + 3) % 4, (y + 2) % 4
    x_up, x_dn = pipe_of(xp, y), pipe_of(xm, y)
    y_up, y_dn = pipe_of(x, yp), pipe_of(x, ym)

    started = []

    def send(src, dst, ss, rs, dev):
        c = pltpu.make_async_remote_copy(
            src_ref=src, dst_ref=dst, send_sem=ss, recv_sem=rs, device_id=dev, device_id_type=MESH
        )
        c.start()
        started.append(c)

    def sent(keep):
        while len(started) > keep:
            started.pop(0).wait_send()

    def arrived(dst, ss, rs, dev):
        pltpu.make_async_remote_copy(
            src_ref=dst, dst_ref=dst, send_sem=ss, recv_sem=rs, device_id=dev, device_id_type=MESH
        ).wait_recv()

    in_enc = pltpu.make_async_copy(enc_ref, enc_buf.at[:, pipe], loc.at[0])
    in_w = pltpu.make_async_copy(w_ref, w_st, loc.at[1])
    in_q = pltpu.make_async_copy(q_ref, q_v, loc.at[2])
    in_cg = pltpu.make_async_copy(cg_ref, cg_v, loc.at[3])
    in_enc.start()
    in_w.start()
    in_q.start()
    in_cg.start()

    barrier = pltpu.get_barrier_semaphore()
    for dev in (far, near, mate, twin, x_up, x_dn, y_up, y_dn):
        pl.semaphore_signal(barrier, inc=1, device_id=dev, device_id_type=MESH)
    pl.semaphore_wait(barrier, 8)

    groups = [("a", 0, 2), ("a", 2, 2), ("b", 4, 1), ("b", 5, 1), ("b", 6, 1), ("b", 7, 1)]

    def piece(g, zz):
        kind, h0, n = groups[g]
        if kind == "a":
            return wb.at[pl.ds(h0, n), core, row, zz]
        return wb.at[h0, core, :, zz]

    def rearrange(h):
        wb[h, core, row, z, :, :HD] = w_st[:, h * HD : (h + 1) * HD]
        wb[h, core, row, z, :, HD:] = w_st[:, (HEADS + h) * HD : (HEADS + h + 1) * HD]

    def mate_send(k, src):
        send(src, src, wy_s.at[k], wy_r.at[k], mate)

    def spread(g, k, zz):
        if g == 0:
            mate_send(k, piece(0, zz))
        if g == 5:
            p = piece(g, zz)
            send(p, p, sib_s.at[10 + k], sib_r.at[10 + k], twin)

    def far_step(g, k):
        p = piece(g, at_z(-k))
        if k >= 1:
            arrived(p, ring_s.at[g, k - 1], ring_r.at[g, k - 1], near)
        elif g < 2:
            for h in range(2 * g, 2 * g + 2):
                rearrange(h)
        if k <= 3:
            send(p, p, ring_s.at[g, k], ring_r.at[g, k], far)
        spread(g, k, at_z(-k))

    def near_step(g, k):
        p = piece(g, at_z(k))
        if k >= 1:
            arrived(p, ring_s.at[g, 3 + k], ring_r.at[g, 3 + k], far)
        if k <= 2:
            send(p, p, ring_s.at[g, 4 + k], ring_r.at[g, 4 + k], near)
        if k >= 1:
            spread(g, 4 + k, at_z(k))

    def group_end(g):
        kind, h0, n = groups[g]
        if g < 5:
            p = wb.at[pl.ds(h0, n), core, row] if kind == "a" else wb.at[h0, core]
            send(p, p, sib_s.at[g], sib_r.at[g], twin)

    def mate_bulk(h, i):
        mate_send(6 + 2 * h + i, wb.at[h, core, row, pl.ds(4 * i, 4)])

    def mate_b():
        for h in range(4, 8):
            rearrange(h)
        mate_send(14, wb.at[pl.ds(4, 4), core, row, z])

    def mate_b_in():
        arrived(wb.at[pl.ds(4, 4), core, orow, z], wy_s.at[14], wy_r.at[14], mate)

    def mate_done(h, i):
        if h == 0:
            for j in range(8):
                zz = at_z(-j) if j <= 4 else at_z(j - 4)
                arrived(wb.at[pl.ds(0, 2), core, orow, zz], wy_s.at[j], wy_r.at[j], mate)
            p = wb.at[pl.ds(0, 2), core, orow]
        else:
            p = wb.at[h, core, orow, pl.ds(4 * i, 4)]
            arrived(p, wy_s.at[6 + 2 * h + i], wy_r.at[6 + 2 * h + i], mate)
        send(p, p, sib_s.at[18 + 2 * h + i], sib_r.at[18 + 2 * h + i], twin)

    oc = 1 - core

    def twin_own(g):
        kind, h0, n = groups[g]
        if kind == "a":
            p = wb.at[pl.ds(h0, n), oc, row]
        else:
            p = wb.at[h0, oc]
        arrived(p, sib_s.at[g], sib_r.at[g], twin)

    def twin_done(h):
        if h < 2:
            if "pair" not in owned:
                owned.add("pair")
                arrived(wb.at[pl.ds(0, 2), oc, orow], sib_s.at[18], sib_r.at[18], twin)
        elif h < 4:
            for i in range(2):
                k = 18 + 2 * h + i
                arrived(wb.at[h, oc, orow, pl.ds(4 * i, 4)], sib_s.at[k], sib_r.at[k], twin)
        elif h < 7:
            twin_own(h - 2)
        else:
            for k in range(8):
                zz = at_z(k) if k <= 4 else at_z(4 - k)
                arrived(wb.at[7, oc, :, zz], sib_s.at[10 + k], sib_r.at[10 + k], twin)

    def enc_x(yy, i):
        b = enc_buf.at[:, x * 4 + yy]
        send(b, b, enc_s.at[4 + i], enc_r.at[4 + i], x_up)
        send(b, b, enc_s.at[8 + i], enc_r.at[8 + i], x_dn)

    def enc_x2(yy, i):
        b = enc_buf.at[:, xm * 4 + yy]
        arrived(b, enc_s.at[4 + i], enc_r.at[4 + i], x_dn)
        b = b.at[0]
        send(b, b, enc_s.at[12 + i], enc_r.at[12 + i], x_up)
        b = enc_buf.at[:, xp * 4 + yy]
        arrived(b, enc_s.at[8 + i], enc_r.at[8 + i], x_up)
        b = b.at[1]
        send(b, b, enc_s.at[16 + i], enc_r.at[16 + i], x_dn)

    def enc_0():
        b = enc_buf.at[:, pipe]
        send(b, b, enc_s.at[0], enc_r.at[0], y_up)
        send(b, b, enc_s.at[1], enc_r.at[1], y_dn)
        enc_x(y, 0)

    def enc_1():
        b = enc_buf.at[:, x * 4 + ym]
        arrived(b, enc_s.at[0], enc_r.at[0], y_dn)
        b = b.at[0]
        send(b, b, enc_s.at[2], enc_r.at[2], y_up)
        b = enc_buf.at[:, x * 4 + yp]
        arrived(b, enc_s.at[1], enc_r.at[1], y_up)
        b = b.at[1]
        send(b, b, enc_s.at[3], enc_r.at[3], y_dn)
        enc_x(ym, 1)
        enc_x(yp, 2)

    def enc_2():
        arrived(enc_buf.at[0, x * 4 + yo], enc_s.at[2], enc_r.at[2], y_dn)
        arrived(enc_buf.at[1, x * 4 + yo], enc_s.at[3], enc_r.at[3], y_up)
        enc_x(yo, 3)

    def enc_end():
        for i, yy in enumerate((y, ym, yp, yo)):
            arrived(enc_buf.at[0, xo * 4 + yy], enc_s.at[12 + i], enc_r.at[12 + i], x_dn)
            arrived(enc_buf.at[1, xo * 4 + yy], enc_s.at[16 + i], enc_r.at[16 + i], x_up)

    def transpose(c):
        b = enc_buf[c // 2, (c % 2) * 8 : (c % 2) * 8 + 8]
        enc_t[:, c * 512 : (c + 1) * 512] = b.reshape(512, TOK).T

    def project(hs):
        for n, h in enumerate(hs):
            kv_v[n] = nn(enc_t[...], wb[h].reshape(WIDTH, 2 * HD)).astype(BF16)

    def attend(*hs):
        at = [
            (n, slice(i * SEQ, (i + 1) * SEQ), slice(h * HD, (h + 1) * HD))
            for n, h in enumerate(hs)
            for i in range(TOK // SEQ)
        ]
        k = [kv_v[n, r, :HD] for n, r, _ in at]
        v = [kv_v[n, r, HD:] for n, r, _ in at]
        q = [q_v[r, c] for _, r, c in at]
        cg = [cg_v[r, c] for _, r, c in at]
        s = [nt(a, b) for a, b in zip(k, q)]
        gp = [nt(a, b) for a, b in zip(v, cg)]
        e = [jnp.exp(t - jnp.max(t, axis=0, keepdims=True)) for t in s]
        p = [t * (1.0 / jnp.sum(t, axis=0, keepdims=True)) for t in e]
        pb = [t.astype(BF16) for t in p]
        gs = [(a * (b - jnp.sum(b * a, axis=0, keepdims=True))).astype(BF16) for a, b in zip(p, gp)]
        for i, (n, r, c) in enumerate(at):
            gkv_v[n, r, :HD] = nn(gs[i], q[i]).astype(BF16)
            gkv_v[n, r, HD:] = nn(pb[i], cg[i]).astype(BF16)
        for i, (n, r, c) in enumerate(at):
            ctx_v[r, c] = tn(pb[i], v[i]).astype(BF16)

    def grad(*hs):
        for c in range(4):
            j, r = c // 2, c % 2
            t = sum(nt(wb[h, j, r].reshape(512, 2 * HD), gkv_v[n]) for n, h in enumerate(hs))
            t = t.reshape(NZ, 64, TOK)
            acc[j, r] = t if first[0] else acc[j, r] + t
        first[0] = False

    first = [True]

    def own_start():
        in_enc.wait()
        enc_0()
        in_w.wait()

    def enc_hop(i):
        enc_x2((y, ym, yp, yo)[i], i)

    def enc_all():
        enc_end()
        in_q.wait()
        in_cg.wait()

    owned = set()

    def project_step(*hs):
        for h in hs:
            if h < 4 and h // 2 not in owned:
                owned.add(h // 2)
                twin_own(h // 2)
            twin_done(h)
        project(hs)

    steps = {
        "e0": own_start, "e1": enc_1, "e2": enc_2, "ex": enc_hop, "ee": enc_all, "t": transpose,
        "yb": mate_b, "ybw": mate_b_in, "F": far_step, "N": near_step, "end": group_end,
        "ys": mate_bulk, "yd": mate_done, "P": project_step, "A": attend, "G": grad,
    }
    for name, *at in ORDER:
        if name == "P":
            sent(KEEP)
        steps[name](*at)

    out_ctx = pltpu.make_async_copy(ctx_v, ctx_ref, loc.at[4])
    out_ctx.start()
    final = [at for name, *at in ORDER if name == "P"][-1]
    g_last = [gkv_v[n] for n in range(len(final))]
    order = (yo, yp, ym, y)

    def blocks(ref, j, xx):
        return ref.at[j, xx // 2, pl.ds((xx % 2) * 4, 4)]

    def last(j, xx):
        t = sum(nt(blocks(wb.at[h], j, xx)[...].reshape(TOK, 2 * HD), g) for h, g in zip(final, g_last))
        return blocks(acc, j, xx)[...] + t.reshape(4, 64, TOK)

    def one(j, xx, yy):
        return acc.at[j, xx // 2, (xx % 2) * 4 + yy]

    def gx(m, r):
        send(xs.at[m, order[r]], xr.at[m, order[r]], gx_s.at[m, r], gx_r.at[m, r], x_up if m % 2 == 0 else x_dn)

    def gx_in(m, r):
        dev = x_dn if m % 2 == 0 else x_up
        arrived(xr.at[m, order[r]], gx_s.at[m, r], gx_r.at[m, r], dev)
        return xr[m, order[r]].astype(F32)

    def relay(r):
        xs[4, order[r]] = (gx_in(0, r) + one(0, xp, order[r])[...]).astype(BF16)
        gx(4, r)
        xs[5, order[r]] = (gx_in(1, r) + one(1, xm, order[r])[...]).astype(BF16)
        gx(5, r)

    def pair(m, r):
        gx(m, r)
        gx(m + 1, r)

    xs[0] = last(0, xo).astype(BF16)
    xs[1] = last(1, xo).astype(BF16)
    pair(0, 0)
    xs[2] = last(1, xp).astype(BF16)
    xs[3] = last(0, xm).astype(BF16)
    pair(2, 0)
    pair(0, 1)
    pair(0, 2)
    sent(8)
    blocks(acc, 0, xp)[...] = last(0, xp)
    blocks(acc, 1, xm)[...] = last(1, xm)
    relay(0)
    pair(2, 1)
    blocks(acc, 0, x)[...] = last(0, x)
    blocks(acc, 1, x)[...] = last(1, x)
    relay(1)
    pair(2, 2)
    relay(2)
    pair(0, 3)
    pair(2, 3)

    def total(r):
        t1 = one(1, x, order[r])[...] + gx_in(2, r)
        t0 = one(0, x, order[r])[...] + gx_in(3, r)
        return t0 + gx_in(4, r), t1 + gx_in(5, r)

    def gy(m, i, v):
        half = pl.ds(32 * i, 32)
        ys[m, half] = v.astype(BF16)
        dev = y_up if m % 2 == 0 else y_dn
        send(ys.at[m, half], yr.at[m, half], gy_s.at[m, i], gy_r.at[m, i], dev)

    def gy_in(m, i):
        half = pl.ds(32 * i, 32)
        arrived(yr.at[m, half], gy_s.at[m, i], gy_r.at[m, i], y_dn if m % 2 == 0 else y_up)
        return yr[m, half].astype(F32)

    def part(v, i):
        return v[32 * i : 32 * i + 32]

    s0, s1 = total(0)
    for i in range(2):
        gy(0, i, part(s0, i))
        gy(1, i, part(s1, i))
    u0, u1 = total(1)
    for i in range(2):
        gy(2, i, part(u1, i))
    d0, d1 = total(2)
    for i in range(2):
        gy(3, i, part(d0, i))
    relay(3)
    for i in range(2):
        gy(4, i, part(u0, i) + gy_in(0, i))
        gy(5, i, part(d1, i) + gy_in(1, i))
    o0, o1 = total(3)
    for i in range(2):
        half = slice(32 * i, 32 * i + 32)
        ge_ref[0, half] = (part(o0, i) + gy_in(3, i) + gy_in(4, i)).astype(BF16)
        ge_ref[1, half] = (part(o1, i) + gy_in(2, i) + gy_in(5, i)).astype(BF16)

    sent(0)
    out_ctx.wait()


def hand_on(ctx_ref, ge_ref, ctx_out, ge_out, ctx_v, ge_v, sem_in, sem_out):
    rows = TOK // PARTS
    parts = [tuple(r.at[pl.ds(i * rows, rows)] for r in (ctx_ref, ctx_v, ctx_out)) for i in range(PARTS)]
    parts.append((ge_ref, ge_v, ge_out))
    there = [pltpu.make_async_copy(s, v, sem_in.at[i]) for i, (s, v, _) in enumerate(parts)]
    on = [pltpu.make_async_copy(v, d, sem_out.at[i]) for i, (_, v, d) in enumerate(parts)]
    for c in there:
        c.start()
    for a, b in zip(there, on):
        a.wait()
        b.start()
    for c in on:
        c.wait()


def local(encoder_out, key_value_weight, queries, context_gradient):
    any_space = pl.BlockSpec(memory_space=pl.ANY)
    vmem = pl.BlockSpec(memory_space=pltpu.VMEM)
    dma = pltpu.SemaphoreType.DMA
    ctx, ge = pl.pallas_call(
        kernel,
        out_shape=(
            jax.ShapeDtypeStruct((TOK, HEADS * HD), BF16),
            jax.ShapeDtypeStruct((2, 64, TOK), BF16),
        ),
        in_specs=[any_space] * 4,
        out_specs=(any_space, vmem),
        scratch_shapes=[
            pltpu.VMEM((HEADS, 2, 2, NZ, 64, 2 * HD), BF16),
            pltpu.VMEM((64, WIDTH), BF16),
            pltpu.VMEM((2, 16, 64, TOK), BF16),
            pltpu.VMEM((TOK, WIDTH), BF16),
            pltpu.VMEM((2, 2, NZ, 64, TOK), F32),
            pltpu.VMEM((TOK, HEADS * HD), BF16),
            pltpu.VMEM((TOK, HEADS * HD), BF16),
            pltpu.VMEM((TOK, HEADS * HD), BF16),
            pltpu.VMEM((2, TOK, 2 * HD), BF16),
            pltpu.VMEM((2, TOK, 2 * HD), BF16),
            pltpu.VMEM((6, 4, 64, TOK), BF16),
            pltpu.VMEM((6, 4, 64, TOK), BF16),
            pltpu.VMEM((6, 64, TOK), BF16),
            pltpu.VMEM((6, 64, TOK), BF16),
            dma((5,)),
            dma((6, 7)),
            dma((6, 7)),
            dma((15,)),
            dma((15,)),
            dma((26,)),
            dma((26,)),
            dma((20,)),
            dma((20,)),
            dma((6, 4)),
            dma((6, 4)),
            dma((6, 2)),
            dma((6, 2)),
        ],
        compiler_params=pltpu.CompilerParams(
            collective_id=0, has_side_effects=True, vmem_limit_bytes=LIMIT * 1024
        ),
    )(
        encoder_out.reshape(2, 64, TOK),
        key_value_weight[0],
        queries[0],
        context_gradient[0],
    )
    ctx, ge = pl.pallas_call(
        hand_on,
        out_shape=(
            jax.ShapeDtypeStruct((TOK, HEADS * HD), BF16),
            jax.ShapeDtypeStruct((2, 64, TOK), BF16),
        ),
        in_specs=[any_space] * 2,
        out_specs=(any_space, any_space),
        scratch_shapes=[
            pltpu.VMEM((TOK, HEADS * HD), BF16),
            pltpu.VMEM((2, 64, TOK), BF16),
            dma((PARTS + 1,)),
            dma((PARTS + 1,)),
        ],
        compiler_params=pltpu.CompilerParams(vmem_limit_bytes=LIMIT * 1024),
    )(ctx, ge)
    return ctx[None], ge.reshape(2 * 64, TOK)


def solution(mesh):
    return jax.shard_map(
        local,
        mesh=mesh,
        in_specs=(P("pipe", "dp"), P("pipe", "dp", None), P("pipe", "dp", None), P("pipe", "dp", None)),
        out_specs=(P("pipe", "dp", None), P("pipe", "dp")),
        check_vma=False,
    )
```

```python
import jax
import jax.numpy as jnp
from jax import lax
from jax.experimental import pallas as pl
from jax.experimental.pallas import tpu as pltpu
from jax.sharding import PartitionSpec as P

MESH = pl.DeviceIdType.MESH
HEADS = 8
HD = 128
SEQ = 128
TOK = 256
WIDTH = 2048
NZ = 8
KEEP = 16
PARTS = 2
LIMIT = 63488
F32 = jnp.float32
BF16 = jnp.bfloat16

ORDER = [
    ("e0",), ("yb",), ("F", 0, 0), ("N", 0, 0), ("F", 1, 0), ("N", 1, 0), ("F", 0, 1), ("ex", 0), ("N", 0, 1),
    ("F", 1, 1), ("N", 1, 1), ("e1",), ("F", 0, 2), ("N", 0, 2), ("F", 1, 2), ("ybw",), ("F", 2, 0),
    ("N", 2, 0), ("F", 3, 0), ("N", 3, 0), ("F", 4, 0), ("N", 1, 2), ("N", 4, 0), ("ex", 1), ("F", 0, 3),
    ("N", 0, 3), ("ex", 2), ("F", 1, 3), ("F", 2, 1), ("N", 2, 1), ("F", 3, 1), ("N", 3, 1), ("e2",),
    ("F", 4, 1), ("N", 1, 3), ("F", 5, 0), ("N", 5, 0), ("N", 4, 1), ("F", 0, 4), ("end", 0), ("F", 1, 4),
    ("end", 1), ("ys", 2, 0), ("ys", 2, 1), ("ys", 3, 0), ("ex", 3), ("F", 2, 2), ("ys", 3, 1), ("N", 2, 2),
    ("F", 3, 2), ("N", 3, 2), ("yd", 0, 0), ("F", 4, 2), ("ee",), ("t", 0), ("t", 1), ("F", 5, 1), ("t", 2),
    ("t", 3), ("N", 5, 1), ("P", 0, 1), ("N", 4, 2), ("yd", 2, 0), ("F", 2, 3), ("A", 0, 1), ("N", 2, 3),
    ("G", 0, 1), ("F", 3, 3), ("N", 3, 3), ("yd", 2, 1), ("F", 4, 3), ("F", 5, 2), ("N", 5, 2), ("N", 4, 3),
    ("yd", 3, 0), ("F", 2, 4), ("end", 2), ("F", 3, 4), ("end", 3), ("F", 4, 4), ("end", 4), ("F", 5, 3),
    ("P", 2, 4), ("N", 5, 3), ("yd", 3, 1), ("A", 2, 4), ("G", 2, 4), ("P", 5, 6), ("A", 5, 6), ("F", 5, 4),
    ("end", 5), ("G", 5, 6), ("P", 3, 7), ("A", 3, 7),
]


def nt(a, b):
    return lax.dot_general(a, b, (((1,), (1,)), ((), ())), preferred_element_type=F32)


def nn(a, b):
    return lax.dot_general(a, b, (((1,), (0,)), ((), ())), preferred_element_type=F32)


def tn(a, b):
    return lax.dot_general(a, b, (((0,), (0,)), ((), ())), preferred_element_type=F32)


def kernel(
    enc_ref, w_ref, q_ref, cg_ref, ctx_ref, ge_ref,
    wb, w_st, enc_buf, enc_t, acc, q_v, cg_v, ctx_v, kv_v, gkv_v, xs, xr, ys, yr,
    loc, ring_s, ring_r, wy_s, wy_r, sib_s, sib_r, enc_s, enc_r, gx_s, gx_r, gy_s, gy_r,
):
    dp, pipe = lax.axis_index("dp"), lax.axis_index("pipe")
    core, z, row = dp % 2, (dp // 2) % NZ, dp // (2 * NZ)
    x, y = pipe // 4, pipe % 4
    dz = 1 - 2 * core
    orow = 1 - row

    def at_z(k):
        return (z + k * dz + 2 * NZ) % NZ

    def dp_of(r, zz, c):
        return {"dp": (r * NZ + zz) * 2 + c}

    def pipe_of(xx, yy):
        return {"pipe": xx * 4 + yy}

    far, near = dp_of(row, at_z(1), core), dp_of(row, at_z(-1), core)
    mate = dp_of(orow, z, core)
    twin = dp_of(row, z, 1 - core)
    xp, xm, xo = (x + 1) % 4, (x + 3) % 4, (x + 2) % 4
    yp, ym, yo = (y + 1) % 4, (y + 3) % 4, (y + 2) % 4
    x_up, x_dn = pipe_of(xp, y), pipe_of(xm, y)
    y_up, y_dn = pipe_of(x, yp), pipe_of(x, ym)

    started = []

    def send(src, dst, ss, rs, dev):
        c = pltpu.make_async_remote_copy(
            src_ref=src, dst_ref=dst, send_sem=ss, recv_sem=rs, device_id=dev, device_id_type=MESH
        )
        c.start()
        started.append(c)

    def sent(keep):
        while len(started) > keep:
            started.pop(0).wait_send()

    def arrived(dst, ss, rs, dev):
        pltpu.make_async_remote_copy(
            src_ref=dst, dst_ref=dst, send_sem=ss, recv_sem=rs, device_id=dev, device_id_type=MESH
        ).wait_recv()

    in_enc = pltpu.make_async_copy(enc_ref, enc_buf.at[:, pipe], loc.at[0])
    in_w = pltpu.make_async_copy(w_ref, w_st, loc.at[1])
    in_q = pltpu.make_async_copy(q_ref, q_v, loc.at[2])
    in_cg = pltpu.make_async_copy(cg_ref, cg_v, loc.at[3])
    in_enc.start()
    in_w.start()
    in_q.start()
    in_cg.start()

    barrier = pltpu.get_barrier_semaphore()
    for dev in (far, near, mate, twin, x_up, x_dn, y_up, y_dn):
        pl.semaphore_signal(barrier, inc=1, device_id=dev, device_id_type=MESH)
    pl.semaphore_wait(barrier, 8)

    groups = [("a", 0, 2), ("a", 2, 2), ("b", 4, 1), ("b", 5, 1), ("b", 6, 1), ("b", 7, 1)]

    def piece(g, zz):
        kind, h0, n = groups[g]
        if kind == "a":
            return wb.at[pl.ds(h0, n), core, row, zz]
        return wb.at[h0, core, :, zz]

    def rearrange(h):
        wb[h, core, row, z, :, :HD] = w_st[:, h * HD : (h + 1) * HD]
        wb[h, core, row, z, :, HD:] = w_st[:, (HEADS + h) * HD : (HEADS + h + 1) * HD]

    def mate_send(k, src):
        send(src, src, wy_s.at[k], wy_r.at[k], mate)

    def spread(g, k, zz):
        if g == 0:
            mate_send(k, piece(0, zz))
        if g == 5:
            p = piece(g, zz)
            send(p, p, sib_s.at[10 + k], sib_r.at[10 + k], twin)

    def far_step(g, k):
        p = piece(g, at_z(-k))
        if k >= 1:
            arrived(p, ring_s.at[g, k - 1], ring_r.at[g, k - 1], near)
        elif g < 2:
            for h in range(2 * g, 2 * g + 2):
                rearrange(h)
        if k <= 3:
            send(p, p, ring_s.at[g, k], ring_r.at[g, k], far)
        spread(g, k, at_z(-k))

    def near_step(g, k):
        p = piece(g, at_z(k))
        if k >= 1:
            arrived(p, ring_s.at[g, 3 + k], ring_r.at[g, 3 + k], far)
        if k <= 2:
            send(p, p, ring_s.at[g, 4 + k], ring_r.at[g, 4 + k], near)
        if k >= 1:
            spread(g, 4 + k, at_z(k))

    def group_end(g):
        kind, h0, n = groups[g]
        if g < 5:
            p = wb.at[pl.ds(h0, n), core, row] if kind == "a" else wb.at[h0, core]
            send(p, p, sib_s.at[g], sib_r.at[g], twin)

    def mate_bulk(h, i):
        mate_send(6 + 2 * h + i, wb.at[h, core, row, pl.ds(4 * i, 4)])

    def mate_b():
        for h in range(4, 8):
            rearrange(h)
        mate_send(14, wb.at[pl.ds(4, 4), core, row, z])

    def mate_b_in():
        arrived(wb.at[pl.ds(4, 4), core, orow, z], wy_s.at[14], wy_r.at[14], mate)

    def mate_done(h, i):
        if h == 0:
            for j in range(8):
                zz = at_z(-j) if j <= 4 else at_z(j - 4)
                arrived(wb.at[pl.ds(0, 2), core, orow, zz], wy_s.at[j], wy_r.at[j], mate)
            p = wb.at[pl.ds(0, 2), core, orow]
        else:
            p = wb.at[h, core, orow, pl.ds(4 * i, 4)]
            arrived(p, wy_s.at[6 + 2 * h + i], wy_r.at[6 + 2 * h + i], mate)
        send(p, p, sib_s.at[18 + 2 * h + i], sib_r.at[18 + 2 * h + i], twin)

    oc = 1 - core

    def twin_own(g):
        kind, h0, n = groups[g]
        if kind == "a":
            p = wb.at[pl.ds(h0, n), oc, row]
        else:
            p = wb.at[h0, oc]
        arrived(p, sib_s.at[g], sib_r.at[g], twin)

    def twin_done(h):
        if h < 2:
            if "pair" not in owned:
                owned.add("pair")
                arrived(wb.at[pl.ds(0, 2), oc, orow], sib_s.at[18], sib_r.at[18], twin)
        elif h < 4:
            for i in range(2):
                k = 18 + 2 * h + i
                arrived(wb.at[h, oc, orow, pl.ds(4 * i, 4)], sib_s.at[k], sib_r.at[k], twin)
        elif h < 7:
            twin_own(h - 2)
        else:
            for k in range(8):
                zz = at_z(k) if k <= 4 else at_z(4 - k)
                arrived(wb.at[7, oc, :, zz], sib_s.at[10 + k], sib_r.at[10 + k], twin)

    def enc_x(yy, i):
        b = enc_buf.at[:, x * 4 + yy]
        send(b, b, enc_s.at[4 + i], enc_r.at[4 + i], x_up)
        send(b, b, enc_s.at[8 + i], enc_r.at[8 + i], x_dn)

    def enc_x2(yy, i):
        b = enc_buf.at[:, xm * 4 + yy]
        arrived(b, enc_s.at[4 + i], enc_r.at[4 + i], x_dn)
        b = b.at[0]
        send(b, b, enc_s.at[12 + i], enc_r.at[12 + i], x_up)
        b = enc_buf.at[:, xp * 4 + yy]
        arrived(b, enc_s.at[8 + i], enc_r.at[8 + i], x_up)
        b = b.at[1]
        send(b, b, enc_s.at[16 + i], enc_r.at[16 + i], x_dn)

    def enc_0():
        b = enc_buf.at[:, pipe]
        send(b, b, enc_s.at[0], enc_r.at[0], y_up)
        send(b, b, enc_s.at[1], enc_r.at[1], y_dn)
        enc_x(y, 0)

    def enc_1():
        b = enc_buf.at[:, x * 4 + ym]
        arrived(b, enc_s.at[0], enc_r.at[0], y_dn)
        b = b.at[0]
        send(b, b, enc_s.at[2], enc_r.at[2], y_up)
        b = enc_buf.at[:, x * 4 + yp]
        arrived(b, enc_s.at[1], enc_r.at[1], y_up)
        b = b.at[1]
        send(b, b, enc_s.at[3], enc_r.at[3], y_dn)
        enc_x(ym, 1)
        enc_x(yp, 2)

    def enc_2():
        arrived(enc_buf.at[0, x * 4 + yo], enc_s.at[2], enc_r.at[2], y_dn)
        arrived(enc_buf.at[1, x * 4 + yo], enc_s.at[3], enc_r.at[3], y_up)
        enc_x(yo, 3)

    def enc_end():
        for i, yy in enumerate((y, ym, yp, yo)):
            arrived(enc_buf.at[0, xo * 4 + yy], enc_s.at[12 + i], enc_r.at[12 + i], x_dn)
            arrived(enc_buf.at[1, xo * 4 + yy], enc_s.at[16 + i], enc_r.at[16 + i], x_up)

    def transpose(c):
        b = enc_buf[c // 2, (c % 2) * 8 : (c % 2) * 8 + 8]
        enc_t[:, c * 512 : (c + 1) * 512] = b.reshape(512, TOK).T

    def project(hs):
        for n, h in enumerate(hs):
            kv_v[n] = nn(enc_t[...], wb[h].reshape(WIDTH, 2 * HD)).astype(BF16)

    def attend(*hs):
        at = [
            (n, slice(i * SEQ, (i + 1) * SEQ), slice(h * HD, (h + 1) * HD))
            for n, h in enumerate(hs)
            for i in range(TOK // SEQ)
        ]
        k = [kv_v[n, r, :HD] for n, r, _ in at]
        v = [kv_v[n, r, HD:] for n, r, _ in at]
        q = [q_v[r, c] for _, r, c in at]
        cg = [cg_v[r, c] for _, r, c in at]
        s = [nt(a, b) for a, b in zip(k, q)]
        gp = [nt(a, b) for a, b in zip(v, cg)]
        e = [jnp.exp(t - jnp.max(t, axis=0, keepdims=True)) for t in s]
        p = [t * (1.0 / jnp.sum(t, axis=0, keepdims=True)) for t in e]
        pb = [t.astype(BF16) for t in p]
        gs = [(a * (b - jnp.sum(b * a, axis=0, keepdims=True))).astype(BF16) for a, b in zip(p, gp)]
        for i, (n, r, c) in enumerate(at):
            gkv_v[n, r, :HD] = nn(gs[i], q[i]).astype(BF16)
            gkv_v[n, r, HD:] = nn(pb[i], cg[i]).astype(BF16)
        for i, (n, r, c) in enumerate(at):
            ctx_v[r, c] = tn(pb[i], v[i]).astype(BF16)

    def grad(*hs):
        for c in range(4):
            j, r = c // 2, c % 2
            t = sum(nt(wb[h, j, r].reshape(512, 2 * HD), gkv_v[n]) for n, h in enumerate(hs))
            t = t.reshape(NZ, 64, TOK)
            acc[j, r] = t if first[0] else acc[j, r] + t
        first[0] = False

    first = [True]

    def own_start():
        in_enc.wait()
        enc_0()
        in_w.wait()

    def enc_hop(i):
        enc_x2((y, ym, yp, yo)[i], i)

    def enc_all():
        enc_end()
        in_q.wait()
        in_cg.wait()

    owned = set()

    def project_step(*hs):
        for h in hs:
            if h < 4 and h // 2 not in owned:
                owned.add(h // 2)
                twin_own(h // 2)
            twin_done(h)
        project(hs)

    steps = {
        "e0": own_start, "e1": enc_1, "e2": enc_2, "ex": enc_hop, "ee": enc_all, "t": transpose,
        "yb": mate_b, "ybw": mate_b_in, "F": far_step, "N": near_step, "end": group_end,
        "ys": mate_bulk, "yd": mate_done, "P": project_step, "A": attend, "G": grad,
    }
    for name, *at in ORDER:
        if name == "P":
            sent(KEEP)
        steps[name](*at)

    out_ctx = pltpu.make_async_copy(ctx_v, ctx_ref, loc.at[4])
    out_ctx.start()
    final = [at for name, *at in ORDER if name == "P"][-1]
    g_last = [gkv_v[n] for n in range(len(final))]
    order = (yo, yp, ym, y)

    def blocks(ref, j, xx):
        return ref.at[j, xx // 2, pl.ds((xx % 2) * 4, 4)]

    def last(j, xx):
        t = sum(nt(blocks(wb.at[h], j, xx)[...].reshape(TOK, 2 * HD), g) for h, g in zip(final, g_last))
        return blocks(acc, j, xx)[...] + t.reshape(4, 64, TOK)

    def one(j, xx, yy):
        return acc.at[j, xx // 2, (xx % 2) * 4 + yy]

    def gx(m, r):
        send(xs.at[m, order[r]], xr.at[m, order[r]], gx_s.at[m, r], gx_r.at[m, r], x_up if m % 2 == 0 else x_dn)

    def gx_in(m, r):
        dev = x_dn if m % 2 == 0 else x_up
        arrived(xr.at[m, order[r]], gx_s.at[m, r], gx_r.at[m, r], dev)
        return xr[m, order[r]].astype(F32)

    def relay(r):
        xs[4, order[r]] = (gx_in(0, r) + one(0, xp, order[r])[...]).astype(BF16)
        gx(4, r)
        xs[5, order[r]] = (gx_in(1, r) + one(1, xm, order[r])[...]).astype(BF16)
        gx(5, r)

    def pair(m, r):
        gx(m, r)
        gx(m + 1, r)

    xs[0] = last(0, xo).astype(BF16)
    xs[1] = last(1, xo).astype(BF16)
    pair(0, 0)
    xs[2] = last(1, xp).astype(BF16)
    xs[3] = last(0, xm).astype(BF16)
    pair(2, 0)
    pair(0, 1)
    pair(0, 2)
    sent(8)
    blocks(acc, 0, xp)[...] = last(0, xp)
    blocks(acc, 1, xm)[...] = last(1, xm)
    relay(0)
    pair(2, 1)
    blocks(acc, 0, x)[...] = last(0, x)
    blocks(acc, 1, x)[...] = last(1, x)
    relay(1)
    pair(2, 2)
    relay(2)
    pair(0, 3)
    pair(2, 3)

    def total(r):
        t1 = one(1, x, order[r])[...] + gx_in(2, r)
        t0 = one(0, x, order[r])[...] + gx_in(3, r)
        return t0 + gx_in(4, r), t1 + gx_in(5, r)

    def gy(m, i, v):
        half = pl.ds(32 * i, 32)
        ys[m, half] = v.astype(BF16)
        dev = y_up if m % 2 == 0 else y_dn
        send(ys.at[m, half], yr.at[m, half], gy_s.at[m, i], gy_r.at[m, i], dev)

    def gy_in(m, i):
        half = pl.ds(32 * i, 32)
        arrived(yr.at[m, half], gy_s.at[m, i], gy_r.at[m, i], y_dn if m % 2 == 0 else y_up)
        return yr[m, half].astype(F32)

    def part(v, i):
        return v[32 * i : 32 * i + 32]

    s0, s1 = total(0)
    for i in range(2):
        gy(0, i, part(s0, i))
        gy(1, i, part(s1, i))
    u0, u1 = total(1)
    for i in range(2):
        gy(2, i, part(u1, i))
    d0, d1 = total(2)
    for i in range(2):
        gy(3, i, part(d0, i))
    relay(3)
    for i in range(2):
        gy(4, i, part(u0, i) + gy_in(0, i))
        gy(5, i, part(d1, i) + gy_in(1, i))
    o0, o1 = total(3)
    for i in range(2):
        half = slice(32 * i, 32 * i + 32)
        ge_ref[0, half] = (part(o0, i) + gy_in(3, i) + gy_in(4, i)).astype(BF16)
        ge_ref[1, half] = (part(o1, i) + gy_in(2, i) + gy_in(5, i)).astype(BF16)

    sent(0)
    out_ctx.wait()


def hand_on(ctx_ref, ge_ref, ctx_out, ge_out, ctx_v, ge_v, sem_in, sem_out):
    rows = TOK // PARTS
    parts = [tuple(r.at[pl.ds(i * rows, rows)] for r in (ctx_ref, ctx_v, ctx_out)) for i in range(PARTS)]
    parts.append((ge_ref, ge_v, ge_out))
    there = [pltpu.make_async_copy(s, v, sem_in.at[i]) for i, (s, v, _) in enumerate(parts)]
    on = [pltpu.make_async_copy(v, d, sem_out.at[i]) for i, (_, v, d) in enumerate(parts)]
    for c in there:
        c.start()
    for a, b in zip(there, on):
        a.wait()
        b.start()
    for c in on:
        c.wait()


def local(encoder_out, key_value_weight, queries, context_gradient):
    any_space = pl.BlockSpec(memory_space=pl.ANY)
    vmem = pl.BlockSpec(memory_space=pltpu.VMEM)
    dma = pltpu.SemaphoreType.DMA
    ctx, ge = pl.pallas_call(
        kernel,
        out_shape=(
            jax.ShapeDtypeStruct((TOK, HEADS * HD), BF16),
            jax.ShapeDtypeStruct((2, 64, TOK), BF16),
        ),
        in_specs=[any_space] * 4,
        out_specs=(any_space, vmem),
        scratch_shapes=[
            pltpu.VMEM((HEADS, 2, 2, NZ, 64, 2 * HD), BF16),
            pltpu.VMEM((64, WIDTH), BF16),
            pltpu.VMEM((2, 16, 64, TOK), BF16),
            pltpu.VMEM((TOK, WIDTH), BF16),
            pltpu.VMEM((2, 2, NZ, 64, TOK), F32),
            pltpu.VMEM((TOK, HEADS * HD), BF16),
            pltpu.VMEM((TOK, HEADS * HD), BF16),
            pltpu.VMEM((TOK, HEADS * HD), BF16),
            pltpu.VMEM((2, TOK, 2 * HD), BF16),
            pltpu.VMEM((2, TOK, 2 * HD), BF16),
            pltpu.VMEM((6, 4, 64, TOK), BF16),
            pltpu.VMEM((6, 4, 64, TOK), BF16),
            pltpu.VMEM((6, 64, TOK), BF16),
            pltpu.VMEM((6, 64, TOK), BF16),
            dma((5,)),
            dma((6, 7)),
            dma((6, 7)),
            dma((15,)),
            dma((15,)),
            dma((26,)),
            dma((26,)),
            dma((20,)),
            dma((20,)),
            dma((6, 4)),
            dma((6, 4)),
            dma((6, 2)),
            dma((6, 2)),
        ],
        compiler_params=pltpu.CompilerParams(
            collective_id=0, has_side_effects=True, vmem_limit_bytes=LIMIT * 1024
        ),
    )(
        encoder_out.reshape(2, 64, TOK),
        key_value_weight[0],
        queries[0],
        context_gradient[0],
    )
    ctx, ge = pl.pallas_call(
        hand_on,
        out_shape=(
            jax.ShapeDtypeStruct((TOK, HEADS * HD), BF16),
            jax.ShapeDtypeStruct((2, 64, TOK), BF16),
        ),
        in_specs=[any_space] * 2,
        out_specs=(any_space, any_space),
        scratch_shapes=[
            pltpu.VMEM((TOK, HEADS * HD), BF16),
            pltpu.VMEM((2, 64, TOK), BF16),
            dma((PARTS + 1,)),
            dma((PARTS + 1,)),
        ],
        compiler_params=pltpu.CompilerParams(vmem_limit_bytes=LIMIT * 1024),
    )(ctx, ge)
    return ctx[None], ge.reshape(2 * 64, TOK)


def solution(mesh):
    return jax.shard_map(
        local,
        mesh=mesh,
        in_specs=(P("pipe", "dp"), P("pipe", "dp", None), P("pipe", "dp", None), P("pipe", "dp", None)),
        out_specs=(P("pipe", "dp", None), P("pipe", "dp")),
        check_vma=False,
    )
```
